32 devices in a mesh: group: 2 (over y), pos: 8 (over z, x), tile: 2 (over core).
Axes of the slice: x: 2, y: 2, z: 4, core: 2. Of those that a mesh axis runs over, the one named last changes fastest.
Arguments:
- object_field: float32 [2, 2048, 256], P(None, ('group', 'pos')), parts along dimension 1, may hold values from -5 to 5
- probe: float32 [2, 8, 65536], P(None, 'tile'), may hold values from -2.1 to 2.1
- measured: float32 [32, 256, 256], P(('group', 'pos')), parts along dimension 0, may hold values from 0.3 to 12
- offsets: int32 [32, 2], P(('group', 'pos')), parts along dimension 0, may hold values from 0 to 768, as said below
- counts: int32 [16], P(('group', 'pos')), parts along dimension 0, may hold values from 1 to 2, as said below
Outputs:
- object_out: float32 [2, 2048, 256], P(None, ('group', 'pos', 'tile')), parts along dimension 1
- probe_out: float32 [2, 16, 65536], P(None, ('group', 'tile'), 'pos'), parts along dimension 1
The draws below stay inside these ranges and needn't reach their ends.
There are 2 independent parts, one for each index of `group`. The reference program is written for one: setup_inputs(seed, part) draws one part's arguments, and reference() takes and returns one part's arrays. A program takes and returns all parts, laid end to end along the dimension named above; an argument that names none is the same for every part. Nothing has to cross between parts.
Inputs may be any that keep to these rules, and one draw needn't show every extreme that they name: The row offset of slot j lies between (j // 2) * 128 - 256 / 2 and (j // 2) * 128, kept within 0 and 768; the column offset between 0 and 0, so every patch lies inside the object; the first slot has offsets (0, 0) and the last (768, 0). Entry p counts the live slots among slots p * 2 to p * 2 + 1, which are the first ones of that block; entry 0 is 2 and entry 1 is 1.
All inputs are finite; a program needn't handle non-finite values.
Results may differ from the reference program's by a relative error of at most 0.0001.
Values sent between devices are 32-bit elements; how exact they have to be, the bound alone decides.
No kernel may reach another device: no remote copies, remote signals or barrier semaphores. Data moves between devices by JAX's collectives and lax.ppermute only.
A program may use at most 64 MiB of HBM per device.

```python
import math
import jax
import jax.numpy as jnp
from jax import lax

PATCH = 256
MODES = 8
CAP = 2
COLS = 256
STRIP = 128
ROWS = 1024
POSITIONS = 16
N_POS = 8


def draw_offsets(key, part):
    key = jax.random.fold_in(key, 11)
    row_key, col_key = jax.random.split(key)
    slot_ids = jnp.arange(POSITIONS, dtype=jnp.int32)
    owners = slot_ids // CAP
    shifted = jax.random.randint(row_key, (POSITIONS,), 0, PATCH // 2 + 1, dtype=jnp.int32)
    row_vals = jnp.clip(owners * STRIP - PATCH // 2 + shifted, 0, ROWS - PATCH)
    col_vals = jax.random.randint(col_key, (POSITIONS,), 0, COLS - PATCH + 1, dtype=jnp.int32)
    row_vals = row_vals.at[0].set(0).at[POSITIONS - 1].set(ROWS - PATCH)
    col_vals = col_vals.at[0].set(0).at[POSITIONS - 1].set(COLS - PATCH)
    return jnp.stack([row_vals, col_vals], axis=1).astype(jnp.int32)


def draw_counts(key, part):
    key = jax.random.fold_in(key, 13)
    values = jax.random.randint(key, (N_POS,), 1, CAP + 1, dtype=jnp.int32)
    return values.at[0].set(CAP).at[1].set(1).astype(jnp.int32)


def block_scale(rng, shape, pieces, smallest, largest):
    gain, own = 1.0, jax.random.fold_in(rng, 6)
    for dim, blocks in pieces:
        draws = jnp.exp(jax.random.uniform(jax.random.fold_in(own, dim), (blocks,), jnp.float32, smallest / len(pieces), largest / len(pieces)))
        gain = gain * jnp.repeat(draws, shape[dim] // blocks).reshape([-1 if axis == dim else 1 for axis in range(len(shape))])
    return gain


def bell_draw(key, extent, deviation, limit, cuts=(), held_as=jnp.bfloat16):
    drawn = deviation * jax.random.normal(key, extent, jnp.float32)
    if cuts:
        drawn = drawn * block_scale(key, extent, cuts, -0.22, 0.18)
    return jnp.clip(drawn, -limit, limit).astype(held_as)


def setup_inputs(seed: int = 0, part: int = 0) -> dict:
    seeds = jax.random.split(jax.random.key(seed), 6)
    part_splits = jax.random.split(jax.random.fold_in(seeds[5], part), 6)
    object_field = bell_draw(part_splits[0], (2, ROWS, COLS), 0.7, 5.0, ((1, 8),), jnp.float32)
    probe = bell_draw(seeds[1], (2, MODES, PATCH * PATCH), 0.35, 2.1, ((1, 2),), jnp.float32)
    measured = jnp.clip(jnp.exp(math.log(12.0) - 3.6888794 * jax.random.uniform(part_splits[2], (POSITIONS, PATCH, PATCH), jnp.float32) ** block_scale(part_splits[2], (POSITIONS, PATCH, PATCH), ((0, 8),), -0.2, 0.2)), 0.3, 12.0)
    offsets = draw_offsets(jax.random.fold_in(jax.random.fold_in(seeds[5], part), 71), part)
    counts = draw_counts(jax.random.fold_in(jax.random.fold_in(seeds[5], part), 71), part)
    return {"object_field": object_field, "probe": probe, "measured": measured, "offsets": offsets, "counts": counts}


damping_factor = 0.1
object_step = 0.5
probe_step = 0.05

def reference(object_field, probe, measured, offsets, counts):
    field = lax.complex(object_field[0], object_field[1])
    probe_grid = lax.complex(probe[0], probe[1]).reshape(MODES, PATCH, PATCH)
    slot_ids = jnp.arange(POSITIONS, dtype=jnp.int32)
    active = (slot_ids % CAP < counts[slot_ids // CAP]).astype(jnp.float32)

    def visit(carry, position_entry):
        grad_real, grad_imag, probe_real, probe_imag = carry
        row_begin, column_begin, measured_intensity, mode_weight = position_entry
        patch = lax.dynamic_slice(field, (row_begin, column_begin), (PATCH, PATCH))
        far = jnp.fft.fft2(probe_grid * patch[None], norm='ortho')
        model_intensity = lax.optimization_barrier(jnp.sum(jnp.real(far) ** 2 + jnp.imag(far) ** 2, axis=0))
        modulus_ratio = (jnp.sqrt(measured_intensity + damping_factor) / jnp.sqrt(model_intensity + damping_factor) - 1.0) * mode_weight
        chi_field = jnp.fft.ifft2(far * modulus_ratio[None], norm='ortho')
        update = lax.optimization_barrier(jnp.sum(jnp.conj(probe_grid) * chi_field, axis=0))
        corner = (row_begin, column_begin)
        current_real = lax.dynamic_slice(grad_real, corner, (PATCH, PATCH))
        current_imag = lax.dynamic_slice(grad_imag, corner, (PATCH, PATCH))
        grad_real = lax.dynamic_update_slice(grad_real, current_real + jnp.real(update), corner)
        grad_imag = lax.dynamic_update_slice(grad_imag, current_imag + jnp.imag(update), corner)
        probe_term = jnp.conj(patch)[None] * chi_field
        return ((grad_real, grad_imag, probe_real + jnp.real(probe_term), probe_imag + jnp.imag(probe_term)), None)
    start = (jnp.zeros((ROWS, COLS), jnp.float32), jnp.zeros((ROWS, COLS), jnp.float32), jnp.zeros((MODES, PATCH, PATCH), jnp.float32), jnp.zeros((MODES, PATCH, PATCH), jnp.float32))
    items = (offsets[:, 0].astype(jnp.int32), offsets[:, 1].astype(jnp.int32), measured, active)
    final, _ = lax.scan(visit, start, items)
    grad_real, grad_imag, probe_real, probe_imag = final
    object_out = object_field + object_step * jnp.stack([grad_real, grad_imag])
    probe_terms = jnp.stack([probe_real, probe_imag]).reshape(2, MODES, PATCH * PATCH)
    probe_out = probe + probe_step * probe_terms
    return (object_out, probe_out)
```

```python
import functools
import math

import jax
import jax.numpy as jnp
import ml_dtypes
import numpy as np
from jax import lax
from jax.experimental import pallas as pl
from jax.experimental.pallas import tpu as pltpu
from jax.sharding import PartitionSpec as P

damping_factor = 0.1
object_step = 0.5
probe_step = 0.05

F32 = jnp.float32
BF16 = jnp.bfloat16
VMEM_LIMIT = 48 * 1024 * 1024


def real_tables(size):
    half = size // 2
    counter = np.arange(half)
    phase = np.outer(counter, counter) % half
    even = np.exp(-2j * np.pi * phase / half) / math.sqrt(size)
    odd = even * np.exp(-2j * np.pi * counter / size)[:, None]
    tables = []
    for matrix in (even, odd):
        real = np.block([[matrix.real, matrix.imag], [-matrix.imag, matrix.real]])
        for form in (real, real.T):
            high = form.astype(ml_dtypes.bfloat16)
            low = (form - high.astype(np.float64)).astype(ml_dtypes.bfloat16)
            tables += [high, low]
    return np.stack(tables).reshape(2, 2, 2, size, size)


def split(value):
    high = value.astype(BF16)
    return high, (value - high.astype(F32)).astype(BF16)


def product(left, right):
    return jnp.dot(left, right, preferred_element_type=F32)


def times_table(value, table):
    high, low = split(value)
    return product(high, table[0]) + product(high, table[1]) + product(low, table[0])


def table_times(table, value):
    high, low = split(value)
    return product(table[0], high) + product(table[1], high) + product(table[0], low)


def forward_wave(real, imag, tables):
    half = real.shape[1] // 2
    row_even, row_odd, col_even, col_odd = tables
    evens = times_table(
        jnp.concatenate([real[:, :half] + real[:, half:], imag[:, :half] + imag[:, half:]], 1),
        row_even,
    )
    odds = times_table(
        jnp.concatenate([real[:, :half] - real[:, half:], imag[:, :half] - imag[:, half:]], 1),
        row_odd,
    )
    real = jnp.concatenate([evens[:, :half], odds[:, :half]], 1)
    imag = jnp.concatenate([evens[:, half:], odds[:, half:]], 1)
    far_even = table_times(
        col_even,
        jnp.concatenate([real[:half] + real[half:], imag[:half] + imag[half:]], 0),
    )
    far_odd = table_times(
        col_odd,
        jnp.concatenate([real[:half] - real[half:], imag[:half] - imag[half:]], 0),
    )
    return far_even, far_odd


def inverse_wave(far_even, far_odd, tables):
    half = far_even.shape[0] // 2
    row_even, row_odd, col_even, col_odd = tables
    evens = table_times(row_even, far_even)
    odds = table_times(row_odd, far_odd)
    real = jnp.concatenate([evens[:half] + odds[:half], evens[:half] - odds[:half]], 0)
    imag = jnp.concatenate([evens[half:] + odds[half:], evens[half:] - odds[half:]], 0)
    evens = times_table(jnp.concatenate([real[:, :half], imag[:, :half]], 1), col_even)
    odds = times_table(jnp.concatenate([real[:, half:], imag[:, half:]], 1), col_odd)
    real = jnp.concatenate(
        [evens[:, :half] + odds[:, :half], evens[:, :half] - odds[:, :half]], 1
    )
    imag = jnp.concatenate(
        [evens[:, half:] + odds[:, half:], evens[:, half:] - odds[:, half:]], 1
    )
    return real, imag


def load_tables(table_ref):
    return tuple(
        (table_ref[parity, form, 0], table_ref[parity, form, 1])
        for form in (0, 1)
        for parity in (0, 1)
    )


def pieces_of(value):
    high, middle = split(value)
    low = (value - high.astype(F32) - middle.astype(F32)).astype(BF16)
    return high, middle, low


def order_kernel(measured_ref, order_ref, out_ref):
    half = order_ref.shape[1] // 2
    columns, rows = order_ref[0], order_ref[1]
    for slot in range(measured_ref.shape[0]):
        value = jnp.sqrt(measured_ref[slot] + damping_factor)
        value = sum(product(piece, columns) for piece in pieces_of(value))
        value = sum(product(rows, piece) for piece in pieces_of(value))
        out_ref[slot, 0] = value[:half]
        out_ref[slot, 1] = value[half:]


def load_rows(ref, index, begin, count):
    offset = lax.rem(begin, 8)
    span = count + 8
    value = ref[(*index, pl.ds(pl.multiple_of(begin - offset, 8), span))]
    return pltpu.roll(value, lax.rem(span - offset, span), 0)[:count]


def forward_kernel(
    place_ref, own_ref, near_ref, other_ref, probe_ref, table_ref,
    far_ref, power_ref, patch_ref, extended,
):
    rows = own_ref.shape[1]
    size = patch_ref.shape[1]
    start = place_ref[0]
    tile = place_ref[1]
    extended[:, rows : 2 * rows] = own_ref[...]
    extended[tile, :rows] = near_ref[0]
    extended[tile, 2 * rows : 3 * rows] = near_ref[1]
    extended[1 - tile, :rows] = other_ref[0]
    extended[1 - tile, 2 * rows : 3 * rows] = other_ref[1]
    patch_real = load_rows(extended, (0,), start, size)
    patch_imag = load_rows(extended, (1,), start, size)
    patch_ref[0] = patch_real
    patch_ref[1] = patch_imag
    tables = load_tables(table_ref)
    half = size // 2
    for mode in range(probe_ref.shape[1]):
        probe_real = probe_ref[0, mode]
        probe_imag = probe_ref[1, mode]
        pieces = forward_wave(
            probe_real * patch_real - probe_imag * patch_imag,
            probe_real * patch_imag + probe_imag * patch_real,
            tables,
        )
        for parity in (0, 1):
            far = pieces[parity]
            far_ref[mode, parity] = far
            power = far[:half] * far[:half] + far[half:] * far[half:]
            if mode == 0:
                power_ref[parity] = power
            else:
                power_ref[parity] += power


def ratio_kernel(active_ref, amplitude_ref, *refs):
    ratio_ref = refs[-1]
    slots = ratio_ref.shape[0]
    for slot in range(slots):
        model = jnp.sqrt(refs[slot][...] + refs[slots + slot][...] + damping_factor)
        ratio_ref[slot] = (amplitude_ref[slot] / model - 1.0) * active_ref[slot].astype(F32)


def inverse_kernel(modes, first, slots, place_ref, table_ref, ratio_ref, probe_ref, *refs):
    far_refs, patch_refs = refs[:slots], refs[slots : 2 * slots]
    refs = refs[2 * slots :]
    if not first:
        refs = refs[1:]
    grad_ref, keep_ref, send_ref = refs
    inner, outer = place_ref[0], place_ref[1]
    size = probe_ref.shape[2]
    outers, rows = keep_ref.shape[1], keep_ref.shape[3]
    half = size // 2
    tables = load_tables(table_ref)
    for index, mode in enumerate(modes):
        probe_real = probe_ref[0, mode]
        probe_imag = probe_ref[1, mode]
        term_real = term_imag = None
        for slot in range(slots):
            pieces = []
            for parity in (0, 1):
                ratio = ratio_ref[slot, parity]
                far = far_refs[slot][mode, parity]
                pieces.append(jnp.concatenate([far[:half] * ratio, far[half:] * ratio], 0))
            real, imag = inverse_wave(*pieces, tables)
            patch_real = patch_refs[slot][0]
            patch_imag = patch_refs[slot][1]
            grad_real = probe_real * real + probe_imag * imag
            grad_imag = probe_real * imag - probe_imag * real
            if first and index == 0:
                grad_ref[slot, 0] = grad_real
                grad_ref[slot, 1] = grad_imag
            else:
                grad_ref[slot, 0] += grad_real
                grad_ref[slot, 1] += grad_imag
            now_real = patch_real * real + patch_imag * imag
            now_imag = patch_real * imag - patch_imag * real
            if slot == 0:
                term_real, term_imag = now_real, now_imag
            else:
                term_real, term_imag = term_real + now_real, term_imag + now_imag
        for block in range(2 * outers):
            target = lax.rem(block // 2 - outer + outers, outers)
            lines = slice(block * rows, (block + 1) * rows)
            mine = inner == block % 2

            @pl.when(mine)
            def _():
                keep_ref[index, target, 0] = term_real[lines]
                keep_ref[index, target, 1] = term_imag[lines]

            @pl.when(jnp.logical_not(mine))
            def _():
                send_ref[index, target, 0] = term_real[lines]
                send_ref[index, target, 1] = term_imag[lines]


def strip_kernel(place_ref, grad_ref, keep_ref, send_ref, spread):
    slots, _, size, _ = grad_ref.shape
    rows = size // 2
    tile = place_ref[slots]
    half = rows // 2
    spread[:, :, :rows] = jnp.zeros(spread.shape[:2] + (rows, size), F32)
    spread[:, :, rows + size :] = jnp.zeros(spread.shape[:2] + (rows + 8, size), F32)
    spread[:, :, rows : rows + size] = grad_ref[...]
    for part in (0, 1):
        for strip in range(3):
            for ref, which in ((keep_ref, tile), (send_ref, 1 - tile)):
                total = None
                for slot in range(slots):
                    begin = rows - place_ref[slot] + strip * rows + which * half
                    value = load_rows(spread, (slot, part), begin, half)
                    total = value if total is None else total + value
                ref[strip, part] = total


def vmem():
    return pl.BlockSpec(memory_space=pltpu.VMEM)


def smem():
    return pl.BlockSpec(memory_space=pltpu.SMEM)


def params():
    return pltpu.CompilerParams(vmem_limit_bytes=VMEM_LIMIT)


def on_device(object_field, probe, measured, offsets, counts):
    _, strip_rows, columns = object_field.shape
    slots, size, _ = measured.shape
    modes = probe.shape[1]
    positions = lax.axis_size("pos")
    tiles = lax.axis_size("tile")
    position = lax.axis_index("pos")
    tile = lax.axis_index("tile")
    up = [(i, i + 1) for i in range(positions - 1)]
    down = [(i + 1, i) for i in range(positions - 1)]
    swap = [(0, 1), (1, 0)]
    tables = jnp.asarray(real_tables(size))

    component = lax.dynamic_index_in_dim(object_field, tile, 0, keepdims=False)
    low = lax.ppermute(component, "pos", up)
    high = lax.ppermute(component, "pos", down)
    near = jnp.stack([low, high])
    other = lax.ppermute(near, "tile", swap)

    probe_grid = probe.reshape(2, modes, size, size)
    order = np.zeros((size, size), ml_dtypes.bfloat16)
    for parity in (0, 1):
        for index in range(size // 2):
            order[2 * index + parity, parity * (size // 2) + index] = 1
    amplitude = pl.pallas_call(
        order_kernel,
        out_shape=jax.ShapeDtypeStruct((slots, 2, size // 2, size), F32),
        in_specs=[vmem(), vmem()],
        out_specs=vmem(),
        compiler_params=params(),
        name="order",
    )(measured, jnp.asarray(np.stack([order, order.T])))

    starts = offsets[:, 0] - (position * strip_rows - strip_rows)
    far, power, patch = [], [], []
    for slot in range(slots):
        place = jnp.stack([starts[slot], tile]).astype(jnp.int32)
        outs = pl.pallas_call(
            forward_kernel,
            out_shape=(
                jax.ShapeDtypeStruct((modes, 2, size, size), F32),
                jax.ShapeDtypeStruct((2, size // 2, size), F32),
                jax.ShapeDtypeStruct((2, size, size), F32),
            ),
            in_specs=[smem()] + [vmem()] * 5,
            out_specs=(vmem(), vmem(), vmem()),
            scratch_shapes=[pltpu.VMEM((2, 3 * strip_rows + 8, columns), F32)],
            compiler_params=params(),
            name="forward",
        )(place, object_field, near, other, probe_grid, tables)
        far.append(outs[0])
        power.append(outs[1])
        patch.append(outs[2])
    others = [lax.ppermute(value, "tile", swap) for value in power]
    active = (jnp.arange(slots, dtype=jnp.int32) < counts[0]).astype(jnp.int32)
    ratio = pl.pallas_call(
        ratio_kernel,
        out_shape=jax.ShapeDtypeStruct((slots, 2, size // 2, size), F32),
        in_specs=[smem()] + [vmem()] * (1 + 2 * slots),
        out_specs=vmem(),
        compiler_params=params(),
        name="ratio",
    )(active, amplitude, *power, *others)

    outers = positions // 2
    direct = outers <= 4
    block_rows = size // positions
    inner, outer = position % 2, position // 2
    where = jnp.stack([inner, outer]) if direct else jnp.zeros((2,), jnp.int32)
    group = 1
    grad = None
    sums = []
    for begin in range(0, modes, group):
        block_shape = jax.ShapeDtypeStruct((group, outers, 2, block_rows, size), F32)
        grad_shape = jax.ShapeDtypeStruct((slots, 2, size, size), F32)
        first = begin == 0
        arguments = [where.astype(jnp.int32), tables, ratio, probe_grid, *far, *patch]
        if not first:
            arguments.append(grad)
        grad, keep, send = pl.pallas_call(
            functools.partial(inverse_kernel, tuple(range(begin, begin + group)), first, slots),
            out_shape=(grad_shape, block_shape, block_shape),
            in_specs=[smem()] + [vmem()] * (len(arguments) - 1),
            out_specs=(vmem(), vmem(), vmem()),
            input_output_aliases={} if first else {len(arguments) - 1: 0},
            compiler_params=params(),
            name="inverse",
        )(*arguments)
        if direct:
            pair = [(i, i ^ 1) for i in range(positions)]
            got = lax.ppermute(send, "pos", pair)
            both = keep + got
            total = both[:, 0]
            for distance in range(1, outers):
                ring = [(i, (i + 2 * distance) % positions) for i in range(positions)]
                total = total + lax.ppermute(both[:, distance], "pos", ring)
        else:
            both = jnp.stack([keep, send], 2).reshape(group, positions, 2, block_rows, size)
            total = lax.psum_scatter(both, "pos", scatter_dimension=1, tiled=True)[:, 0]
        sums.append(total)

    strip_shape = jax.ShapeDtypeStruct((3, 2, strip_rows // tiles, columns), F32)
    kept, sent = pl.pallas_call(
        strip_kernel,
        out_shape=(strip_shape, strip_shape),
        in_specs=[smem(), vmem()],
        out_specs=(vmem(), vmem()),
        scratch_shapes=[pltpu.VMEM((slots, 2, 2 * strip_rows + size + 8, columns), F32)],
        compiler_params=params(),
        name="strips",
    )(jnp.concatenate([starts, tile[None]]).astype(jnp.int32), grad)
    strips = kept + lax.ppermute(sent, "tile", swap)
    from_above = lax.ppermute(strips[0], "pos", down)
    from_below = lax.ppermute(strips[2], "pos", up)
    half_rows = strip_rows // tiles
    own_rows = lax.dynamic_slice_in_dim(object_field, tile * half_rows, half_rows, 1)
    object_out = own_rows + object_step * (strips[1] + from_above + from_below)

    pixel_share = size * size // positions
    probe_own = lax.dynamic_slice_in_dim(probe, position * pixel_share, pixel_share, 2)
    probe_mine = jnp.concatenate(sums, 0).transpose(1, 0, 2, 3).reshape(2, modes, pixel_share)
    return (object_out, probe_own + probe_step * probe_mine)


def solution(mesh):
    in_specs = (
        P(None, ("group", "pos"), None),
        P(None, "tile", None),
        P(("group", "pos"), None, None),
        P(("group", "pos"), None),
        P(("group", "pos")),
    )
    out_specs = (P(None, ("group", "pos", "tile"), None), P(None, ("group", "tile"), "pos"))
    return jax.shard_map(
        on_device, mesh=mesh, in_specs=in_specs, out_specs=out_specs, check_vma=False
    )
```

```python
import functools
import math

import jax
import jax.numpy as jnp
import ml_dtypes
import numpy as np
from jax import lax
from jax.experimental import pallas as pl
from jax.experimental.pallas import tpu as pltpu
from jax.sharding import PartitionSpec as P

damping_factor = 0.1
object_step = 0.5
probe_step = 0.05

F32 = jnp.float32
BF16 = jnp.bfloat16
VMEM_LIMIT = 24 * 1024 * 1024


def real_tables(size):
    half = size // 2
    counter = np.arange(half)
    phase = np.outer(counter, counter) % half
    even = np.exp(-2j * np.pi * phase / half) / math.sqrt(size)
    odd = even * np.exp(-2j * np.pi * counter / size)[:, None]
    tables = []
    for matrix in (even, odd):
        real = np.block([[matrix.real, matrix.imag], [-matrix.imag, matrix.real]])
        for form in (real, real.T):
            high = form.astype(ml_dtypes.bfloat16)
            low = (form - high.astype(np.float64)).astype(ml_dtypes.bfloat16)
            tables += [high, low]
    return np.stack(tables).reshape(2, 2, 2, size, size)


def split(value):
    high = value.astype(BF16)
    return high, (value - high.astype(F32)).astype(BF16)


def product(left, right):
    return jnp.dot(left, right, preferred_element_type=F32)


def times_table(value, table):
    high, low = split(value)
    return product(high, table[0]) + product(high, table[1]) + product(low, table[0])


def table_times(table, value):
    high, low = split(value)
    return product(table[0], high) + product(table[1], high) + product(table[0], low)


def forward_wave(real, imag, tables):
    half = real.shape[1] // 2
    row_even, row_odd, col_even, col_odd = tables
    evens = times_table(
        jnp.concatenate([real[:, :half] + real[:, half:], imag[:, :half] + imag[:, half:]], 1),
        row_even,
    )
    odds = times_table(
        jnp.concatenate([real[:, :half] - real[:, half:], imag[:, :half] - imag[:, half:]], 1),
        row_odd,
    )
    real = jnp.concatenate([evens[:, :half], odds[:, :half]], 1)
    imag = jnp.concatenate([evens[:, half:], odds[:, half:]], 1)
    far_even = table_times(
        col_even,
        jnp.concatenate([real[:half] + real[half:], imag[:half] + imag[half:]], 0),
    )
    far_odd = table_times(
        col_odd,
        jnp.concatenate([real[:half] - real[half:], imag[:half] - imag[half:]], 0),
    )
    return far_even, far_odd


def inverse_wave(far_even, far_odd, tables):
    half = far_even.shape[0] // 2
    row_even, row_odd, col_even, col_odd = tables
    evens = table_times(row_even, far_even)
    odds = table_times(row_odd, far_odd)
    real = jnp.concatenate([evens[:half] + odds[:half], evens[:half] - odds[:half]], 0)
    imag = jnp.concatenate([evens[half:] + odds[half:], evens[half:] - odds[half:]], 0)
    evens = times_table(jnp.concatenate([real[:, :half], imag[:, :half]], 1), col_even)
    odds = times_table(jnp.concatenate([real[:, half:], imag[:, half:]], 1), col_odd)
    real = jnp.concatenate(
        [evens[:, :half] + odds[:, :half], evens[:, :half] - odds[:, :half]], 1
    )
    imag = jnp.concatenate(
        [evens[:, half:] + odds[:, half:], evens[:, half:] - odds[:, half:]], 1
    )
    return real, imag


def load_tables(table_ref):
    return tuple(
        (table_ref[parity, form, 0], table_ref[parity, form, 1])
        for form in (0, 1)
        for parity in (0, 1)
    )


def pieces_of(value):
    high, middle = split(value)
    low = (value - high.astype(F32) - middle.astype(F32)).astype(BF16)
    return high, middle, low


def prepare_kernel(place_ref, probe_ref, measured_ref, order_ref, grid_ref, own_ref, out_ref):
    parts, modes, size, columns = grid_ref.shape
    lines = columns // 128
    for part in range(parts):
        for mode in range(modes):
            for line in range(lines):
                grid_ref[part, mode, :, line * 128 : (line + 1) * 128] = probe_ref[
                    part, pl.ds(line * modes + mode, size, stride=lines * modes), :
                ]
    share = own_ref.shape[1]
    own_ref[...] = probe_ref[:, pl.ds(pl.multiple_of(place_ref[0] * share, share), share), :]
    half = order_ref.shape[1] // 2
    columns, rows = order_ref[0], order_ref[1]
    for slot in range(measured_ref.shape[0]):
        value = jnp.sqrt(measured_ref[slot] + damping_factor)
        value = sum(product(piece, columns) for piece in pieces_of(value))
        value = sum(product(rows, piece) for piece in pieces_of(value))
        out_ref[slot, 0] = value[:half]
        out_ref[slot, 1] = value[half:]


def load_rows(ref, index, begin, count):
    offset = lax.rem(begin, 8)
    span = count + 8
    value = ref[(*index, pl.ds(pl.multiple_of(begin - offset, 8), span))]
    return pltpu.roll(value, lax.rem(span - offset, span), 0)[:count]


def forward_kernel(
    place_ref, own_ref, near_ref, other_ref, probe_ref, table_ref,
    far_ref, power_ref, patch_ref, extended,
):
    rows = own_ref.shape[1]
    size = patch_ref.shape[1]
    start = place_ref[0]
    tile = place_ref[1]
    extended[:, rows : 2 * rows] = own_ref[...]
    extended[tile, :rows] = near_ref[0]
    extended[tile, 2 * rows : 3 * rows] = near_ref[1]
    extended[1 - tile, :rows] = other_ref[0]
    extended[1 - tile, 2 * rows : 3 * rows] = other_ref[1]
    patch_real = load_rows(extended, (0,), start, size)
    patch_imag = load_rows(extended, (1,), start, size)
    patch_ref[0] = patch_real
    patch_ref[1] = patch_imag
    tables = load_tables(table_ref)
    half = size // 2
    for mode in range(probe_ref.shape[1]):
        probe_real = probe_ref[0, mode]
        probe_imag = probe_ref[1, mode]
        pieces = forward_wave(
            probe_real * patch_real - probe_imag * patch_imag,
            probe_real * patch_imag + probe_imag * patch_real,
            tables,
        )
        for parity in (0, 1):
            far = pieces[parity]
            far_ref[mode, parity] = far
            power = far[:half] * far[:half] + far[half:] * far[half:]
            if mode == 0:
                power_ref[parity] = power
            else:
                power_ref[parity] += power


def inverse_kernel(modes, first, slots, place_ref, table_ref, probe_ref, *refs):
    far_refs, patch_refs = refs[:slots], refs[slots : 2 * slots]
    refs = refs[2 * slots :]
    if first:
        amplitude_ref, power_refs, other_refs = refs[0], refs[1 : 1 + slots], refs[1 + slots : 1 + 2 * slots]
        grad_ref, keep_ref, send_ref, ratio_ref = refs[1 + 2 * slots :]
        for slot in range(slots):
            model = jnp.sqrt(power_refs[slot][...] + other_refs[slot][...] + damping_factor)
            active = (slot < place_ref[2]).astype(F32)
            ratio_ref[slot] = (amplitude_ref[slot] / model - 1.0) * active
    else:
        _, ratio_ref, grad_ref, keep_ref, send_ref = refs
    inner, outer = place_ref[0], place_ref[1]
    size = probe_ref.shape[2]
    outers, rows = keep_ref.shape[1], keep_ref.shape[3]
    half = size // 2
    tables = load_tables(table_ref)
    for index, mode in enumerate(modes):
        probe_real = probe_ref[0, mode]
        probe_imag = probe_ref[1, mode]
        term_real = term_imag = None
        for slot in range(slots):
            pieces = []
            for parity in (0, 1):
                ratio = ratio_ref[slot, parity]
                far = far_refs[slot][mode, parity]
                pieces.append(jnp.concatenate([far[:half] * ratio, far[half:] * ratio], 0))
            real, imag = inverse_wave(*pieces, tables)
            patch_real = patch_refs[slot][0]
            patch_imag = patch_refs[slot][1]
            grad_real = probe_real * real + probe_imag * imag
            grad_imag = probe_real * imag - probe_imag * real
            if first and index == 0:
                grad_ref[slot, 0] = grad_real
                grad_ref[slot, 1] = grad_imag
            else:
                grad_ref[slot, 0] += grad_real
                grad_ref[slot, 1] += grad_imag
            now_real = patch_real * real + patch_imag * imag
            now_imag = patch_real * imag - patch_imag * real
            if slot == 0:
                term_real, term_imag = now_real, now_imag
            else:
                term_real, term_imag = term_real + now_real, term_imag + now_imag
        for block in range(2 * outers):
            target = lax.rem(block // 2 - outer + outers, outers)
            lines = slice(block * rows, (block + 1) * rows)
            mine = inner == block % 2

            @pl.when(mine)
            def _():
                keep_ref[index, target, 0] = term_real[lines]
                keep_ref[index, target, 1] = term_imag[lines]

            @pl.when(jnp.logical_not(mine))
            def _():
                send_ref[index, target, 0] = term_real[lines]
                send_ref[index, target, 1] = term_imag[lines]


def strip_kernel(place_ref, grad_ref, keep_ref, send_ref, spread):
    slots, _, size, _ = grad_ref.shape
    rows = size // 2
    tile = place_ref[slots]
    half = rows // 2
    spread[:, :, :rows] = jnp.zeros(spread.shape[:2] + (rows, size), F32)
    spread[:, :, rows + size :] = jnp.zeros(spread.shape[:2] + (rows + 8, size), F32)
    spread[:, :, rows : rows + size] = grad_ref[...]
    for part in (0, 1):
        for strip in range(3):
            for ref, which in ((keep_ref, tile), (send_ref, 1 - tile)):
                total = None
                for slot in range(slots):
                    begin = rows - place_ref[slot] + strip * rows + which * half
                    value = load_rows(spread, (slot, part), begin, half)
                    total = value if total is None else total + value
                ref[strip, part] = total


def finish_kernel(counts, place_ref, probe_ref, strip_ref, mid_ref, above_ref, below_ref, *refs):
    object_ref, out_ref = refs[-2:]
    half = object_ref.shape[1]
    begin = pl.multiple_of(place_ref[0] * half, half)
    object_ref[...] = strip_ref[:, pl.ds(begin, half), :] + object_step * (
        mid_ref[...] + above_ref[...] + below_ref[...]
    )
    modes = sum(group for group, _ in counts)
    mode = 0
    for group, terms in counts:
        group_refs, refs = refs[:terms], refs[terms:]
        for index in range(group):
            for part in range(out_ref.shape[0]):
                value = sum(ref[index, part] for ref in group_refs)
                rows, columns = value.shape
                lines = columns // 128
                for line in range(lines):
                    where = pl.ds(line * modes + mode, rows, stride=lines * modes)
                    out_ref[part, where, :] = probe_ref[part, where, :] + probe_step * (
                        value[:, line * 128 : (line + 1) * 128]
                    )
            mode += 1


def call(kernel, out_shape, scalars, arrays, name, **options):
    several = isinstance(out_shape, (tuple, list))
    vmem = pl.BlockSpec(memory_space=pltpu.VMEM)
    return pl.pallas_call(
        kernel,
        out_shape=out_shape,
        in_specs=[pl.BlockSpec(memory_space=pltpu.SMEM)] + [vmem] * len(arrays),
        out_specs=(vmem,) * len(out_shape) if several else vmem,
        compiler_params=pltpu.CompilerParams(vmem_limit_bytes=VMEM_LIMIT),
        name=name,
        **options,
    )(jnp.stack(scalars).astype(jnp.int32), *arrays)


def shape(*sizes):
    return jax.ShapeDtypeStruct(sizes, F32)


def on_device(object_field, probe, measured, offsets, counts):
    parts, strip_rows, columns = object_field.shape
    slots, size, _ = measured.shape
    modes = probe.shape[1]
    half = size // 2
    positions = lax.axis_size("pos")
    tiles = lax.axis_size("tile")
    position = lax.axis_index("pos")
    tile = lax.axis_index("tile")
    up = [(i, i + 1) for i in range(positions - 1)]
    down = [(i + 1, i) for i in range(positions - 1)]
    swap = [(0, 1), (1, 0)]
    tables = jnp.asarray(real_tables(size))

    component = lax.dynamic_index_in_dim(object_field, tile, 0, keepdims=False)
    low = lax.ppermute(component, "pos", up)
    high = lax.ppermute(component, "pos", down)

    pixel_lines = size * size // 128
    share = pixel_lines // positions * modes
    order = np.zeros((size, size), ml_dtypes.bfloat16)
    for parity in (0, 1):
        for index in range(half):
            order[2 * index + parity, parity * half + index] = 1
    probe_lines = probe.reshape(parts, modes, pixel_lines, 128).transpose(0, 2, 1, 3)
    probe_grid, probe_own, amplitude = call(
        prepare_kernel,
        (shape(parts, modes, size, size), shape(parts, share, 128), shape(slots, 2, half, size)),
        [position],
        [
            probe_lines.reshape(parts, pixel_lines * modes, 128),
            measured,
            jnp.asarray(np.stack([order, order.T])),
        ],
        "prepare",
    )
    low, high, probe_grid = lax.optimization_barrier((low, high, probe_grid))
    near = jnp.stack([low, high])
    other = lax.ppermute(near, "tile", swap)

    starts = offsets[:, 0] - (position * strip_rows - strip_rows)
    far, power, patch = [], [], []
    for slot in range(slots):
        outs = call(
            forward_kernel,
            (shape(modes, 2, size, size), shape(2, half, size), shape(parts, size, size)),
            [starts[slot], tile],
            [object_field, near, other, probe_grid, tables],
            "forward",
            scratch_shapes=[pltpu.VMEM((parts, 3 * strip_rows + 8, columns), F32)],
        )
        far.append(outs[0])
        power.append(outs[1])
        patch.append(outs[2])
    others = [lax.ppermute(value, "tile", swap) for value in power]

    outers = positions // 2
    direct = outers <= 4
    block_rows = size // positions
    where = [position % 2, position // 2] if direct else [jnp.int32(0), jnp.int32(0)]
    group = 1
    sums = []
    for begin in range(0, modes, group):
        block_shape = shape(group, outers, 2, block_rows, size)
        grad_shape = shape(slots, 2, size, size)
        first = begin == 0
        kernel = functools.partial(
            inverse_kernel, tuple(range(begin, begin + group)), first, slots
        )
        arrays = [tables, probe_grid, *far, *patch]
        if first:
            grad, keep, send, ratio = call(
                kernel,
                (grad_shape, block_shape, block_shape, shape(slots, 2, half, size)),
                [*where, counts[0]],
                [*arrays, amplitude, *power, *others],
                "inverse",
            )
        else:
            arrays += [grad, ratio]
            grad, keep, send = call(
                kernel,
                (grad_shape, block_shape, block_shape),
                where,
                arrays,
                "inverse",
                input_output_aliases={len(arrays) - 1: 0},
            )
        if direct:
            pair = [(i, i ^ 1) for i in range(positions)]
            both = keep + lax.ppermute(send, "pos", pair)
            terms = [both[:, 0]]
            for distance in range(1, outers):
                ring = [(i, (i + 2 * distance) % positions) for i in range(positions)]
                terms.append(lax.ppermute(both[:, distance], "pos", ring))
        else:
            both = jnp.stack([keep, send], 2).reshape(group, positions, 2, block_rows, size)
            terms = [lax.psum_scatter(both, "pos", scatter_dimension=1, tiled=True)[:, 0]]
        sums.append(terms)

    half_rows = strip_rows // tiles
    strip_shape = shape(3, parts, half_rows, columns)
    kept, sent = call(
        strip_kernel,
        (strip_shape, strip_shape),
        [*(starts[slot] for slot in range(slots)), tile],
        [grad],
        "strips",
        scratch_shapes=[pltpu.VMEM((slots, parts, 2 * strip_rows + size + 8, columns), F32)],
    )
    strips = kept + lax.ppermute(sent, "tile", swap)
    above = lax.ppermute(strips[0], "pos", down)
    below = lax.ppermute(strips[2], "pos", up)

    object_out, probe_out = call(
        functools.partial(finish_kernel, [(group, len(terms)) for terms in sums]),
        (shape(parts, half_rows, columns), shape(parts, share, 128)),
        [tile],
        [probe_own, object_field, strips[1], above, below, *sum(sums, [])],
        "finish",
    )
    probe_out = probe_out.reshape(parts, share // modes, modes, 128).transpose(0, 2, 1, 3)
    return (object_out, probe_out.reshape(parts, modes, share // modes * 128))


def solution(mesh):
    in_specs = (
        P(None, ("group", "pos"), None),
        P(None, "tile", None),
        P(("group", "pos"), None, None),
        P(("group", "pos"), None),
        P(("group", "pos")),
    )
    out_specs = (P(None, ("group", "pos", "tile"), None), P(None, ("group", "tile"), "pos"))
    return jax.shard_map(
        on_device, mesh=mesh, in_specs=in_specs, out_specs=out_specs, check_vma=False
    )
```

```python
import functools
import math

import jax
import jax.numpy as jnp
import ml_dtypes
import numpy as np
from jax import lax
from jax.experimental import pallas as pl
from jax.experimental.pallas import tpu as pltpu
from jax.sharding import PartitionSpec as P

damping_factor = 0.1
object_step = 0.5
probe_step = 0.05

F32 = jnp.float32
BF16 = jnp.bfloat16
VMEM_LIMIT = 16 * 1024 * 1024
COSTS = {'prepare': 2000000000, 'forward': 4000000000, 'inverse': 2400000000, 'strips': 1200000000, 'finish': 1000000000, 'order': 1000000000}
CHUNK = 64
TIE = None
GROUPS = ((1, (1, 0, 2)), (1, (0, 1, 2)), (1, (1, 0, 2)), (1, (0, 1, 2)))


def real_tables(size):
    half = size // 2
    counter = np.arange(half)
    phase = np.outer(counter, counter) % half
    even = np.exp(-2j * np.pi * phase / half) / math.sqrt(size)
    odd = even * np.exp(-2j * np.pi * counter / size)[:, None]
    right, left = [], []
    for matrix in (even, odd):
        real = np.block([[matrix.real, matrix.imag], [-matrix.imag, matrix.real]])
        for form in (real, real.T):
            high = form.astype(ml_dtypes.bfloat16)
            low = (form - high.astype(np.float64)).astype(ml_dtypes.bfloat16)
            right.append(np.concatenate([high, high, low], 0))
            left.append(np.concatenate([high, high, low], 1))
    return np.stack(right), np.stack(left)


def split(value):
    high = value.astype(BF16)
    return high, (value - high.astype(F32)).astype(BF16)


def product(left, right):
    return jnp.dot(left, right, preferred_element_type=F32)


def put_left(ref, parity, begin, value):
    size = value.shape[1]
    lines = slice(begin, begin + value.shape[0])
    high, low = split(value)
    ref[parity, lines, :size] = high
    ref[parity, lines, size : 2 * size] = low
    ref[parity, lines, 2 * size :] = high


def put_right(ref, parity, begin, value):
    size = value.shape[1]
    high, low = split(value)
    for index, piece in enumerate((high, low, high)):
        ref[parity, index * size + begin : index * size + begin + value.shape[0]] = piece


def spans(size, count):
    return [(begin, slice(begin, begin + count)) for begin in range(0, size, count)]


def pieces_of(value):
    high, middle = split(value)
    low = (value - high.astype(F32) - middle.astype(F32)).astype(BF16)
    return high, middle, low


def prepare_kernel(probe_ref, grid_ref, own_ref):
    parts, modes, size, columns = grid_ref.shape
    lines = columns // 128
    for part in range(parts):
        for mode in range(modes):
            for line in range(lines):
                grid_ref[part, mode, :, line * 128 : (line + 1) * 128] = probe_ref[
                    part, pl.ds(line * modes + mode, size, stride=lines * modes), :
                ]
    share = own_ref.shape[1]
    own_ref[...] = probe_ref[:, pl.ds(pl.multiple_of(lax.axis_index("pos") * share, share), share), :]


def order_kernel(measured_ref, order_ref, out_ref):
    half = order_ref.shape[1] // 2
    columns, rows = order_ref[0], order_ref[1]
    for slot in range(measured_ref.shape[0]):
        value = jnp.sqrt(measured_ref[slot] + damping_factor)
        value = sum(product(piece, columns) for piece in pieces_of(value))
        value = sum(product(rows, piece) for piece in pieces_of(value))
        out_ref[slot, 0] = value[:half]
        out_ref[slot, 1] = value[half:]


def load_rows(ref, index, begin, count):
    offset = lax.rem(begin, 8)
    span = count + 8
    value = ref[(*index, pl.ds(pl.multiple_of(begin - offset, 8), span))]
    return pltpu.roll(value, lax.rem(span - offset, span), 0)[:count]


def forward_kernel(
    slot, offset_ref, own_ref, pair_ref, next_ref, pair_other_ref, next_other_ref,
    probe_ref, row_ref, col_ref, far_ref, power_ref, patch_ref, extended, left_ref, right_ref,
    middle_ref,
):
    rows = own_ref.shape[1]
    size = patch_ref.shape[1]
    position, tile = lax.axis_index("pos"), lax.axis_index("tile")
    parity = lax.rem(position, 2)
    start = offset_ref[slot, 0] - (position - 1) * rows
    extended[:, rows : 2 * rows] = own_ref[...]
    for side, mine, other in (
        (1 - parity, pair_ref, pair_other_ref),
        (parity, next_ref, next_other_ref),
    ):
        lines = pl.ds(pl.multiple_of(side * (2 * rows), rows), rows)
        extended[tile, lines] = mine[...]
        extended[1 - tile, lines] = other[...]
    for part in (0, 1):
        patch_ref[part] = load_rows(extended, (part,), start, size)
    half = size // 2
    for mode in range(probe_ref.shape[1]):
        for begin, lines in spans(size, CHUNK):
            patch_real, patch_imag = patch_ref[0, lines], patch_ref[1, lines]
            probe_real, probe_imag = probe_ref[0, mode, lines], probe_ref[1, mode, lines]
            real = probe_real * patch_real - probe_imag * patch_imag
            imag = probe_real * patch_imag + probe_imag * patch_real
            a, b = real[:, :half], real[:, half:]
            c, d = imag[:, :half], imag[:, half:]
            put_left(left_ref, 0, begin, jnp.concatenate([a + b, c + d], 1))
            put_left(left_ref, 1, begin, jnp.concatenate([a - b, c - d], 1))
        for parity in (0, 1):
            middle_ref[parity] = product(left_ref[parity], row_ref[2 * parity])
        for begin, lines in spans(half, CHUNK // 2):
            under = slice(half + begin, half + begin + CHUNK // 2)
            for part in (0, 1):
                where = slice(part * half, (part + 1) * half)
                top = jnp.concatenate([middle_ref[0, lines, where], middle_ref[1, lines, where]], 1)
                low = jnp.concatenate([middle_ref[0, under, where], middle_ref[1, under, where]], 1)
                put_right(right_ref, 0, part * half + begin, top + low)
                put_right(right_ref, 1, part * half + begin, top - low)
        for parity in (0, 1):
            far_ref[mode, parity] = product(col_ref[2 * parity + 1], right_ref[parity])
            for begin, lines in spans(half, CHUNK):
                under = slice(half + begin, half + begin + CHUNK)
                real, imag = far_ref[mode, parity, lines], far_ref[mode, parity, under]
                power = real * real + imag * imag
                if mode == 0:
                    power_ref[parity, lines] = power
                else:
                    power_ref[parity, lines] += power


def block_index(block, position, bits):
    index = 0
    for bit in bits:
        differs = lax.rem(lax.div(position, 2**bit) + (block >> bit) % 2, 2)
        index = 2 * index + differs
    return index


def inverse_kernel(modes, bits, first, slots, *refs):
    if first:
        count_ref, *refs = refs
    row_ref, col_ref, probe_ref, *refs = refs
    *refs, left_ref, right_ref, middle_ref = refs
    far_refs, patch_refs = refs[:slots], refs[slots : 2 * slots]
    refs = refs[2 * slots :]
    if first:
        amplitude_ref, power_refs = refs[0], refs[1 : 1 + slots]
        other_refs = refs[1 + slots : 1 + 2 * slots]
        grad_ref, block_ref, ratio_ref = refs[1 + 2 * slots :]
        for slot in range(slots):
            model = jnp.sqrt(power_refs[slot][...] + other_refs[slot][...] + damping_factor)
            active = (slot < count_ref[0]).astype(F32)
            ratio_ref[slot] = (amplitude_ref[slot] / model - 1.0) * active
    else:
        _, ratio_ref, grad_ref, block_ref = refs
    size = probe_ref.shape[2]
    blocks, rows = block_ref.shape[0], block_ref.shape[3]
    half = size // 2
    position = lax.axis_index("pos")
    for index, mode in enumerate(modes):
        for slot in range(slots):
            for begin, lines in spans(half, CHUNK // 2):
                under = slice(half + begin, half + begin + CHUNK // 2)
                for parity in (0, 1):
                    ratio = ratio_ref[slot, parity, lines]
                    far = far_refs[slot].at[mode, parity]
                    put_right(right_ref, parity, begin, far[lines] * ratio)
                    put_right(right_ref, parity, half + begin, far[under] * ratio)
            for parity in (0, 1):
                middle_ref[parity] = product(col_ref[2 * parity], right_ref[parity])
            for begin, lines in spans(half, CHUNK // 2):
                under = slice(half + begin, half + begin + CHUNK // 2)
                for offset, sign in ((0, 1.0), (half, -1.0)):
                    real = middle_ref[0, lines] + sign * middle_ref[1, lines]
                    imag = middle_ref[0, under] + sign * middle_ref[1, under]
                    for parity in (0, 1):
                        where = slice(parity * half, (parity + 1) * half)
                        value = jnp.concatenate([real[:, where], imag[:, where]], 1)
                        put_left(left_ref, parity, offset + begin, value)
            for parity in (0, 1):
                middle_ref[parity] = product(left_ref[parity], row_ref[2 * parity + 1])
            for begin, lines in spans(size, rows):
                target = block_index(begin // rows, position, bits)
                a, b = middle_ref[0, lines], middle_ref[1, lines]
                plus, minus = a + b, a - b
                real = jnp.concatenate([plus[:, :half], minus[:, :half]], 1)
                imag = jnp.concatenate([plus[:, half:], minus[:, half:]], 1)
                probe_real, probe_imag = probe_ref[0, mode, lines], probe_ref[1, mode, lines]
                patch_real, patch_imag = patch_refs[slot][0, lines], patch_refs[slot][1, lines]
                grads = (
                    probe_real * real + probe_imag * imag,
                    probe_real * imag - probe_imag * real,
                )
                terms = (
                    patch_real * real + patch_imag * imag,
                    patch_real * imag - patch_imag * real,
                )
                for part in (0, 1):
                    if first and index == 0:
                        grad_ref[slot, part, lines] = grads[part]
                    else:
                        grad_ref[slot, part, lines] += grads[part]
                    if slot == 0:
                        block_ref[target, index, part] = terms[part]
                    else:
                        block_ref[target, index, part] += terms[part]


def strip_kernel(offset_ref, grad_ref, keep_ref, send_ref, spread):
    slots, _, size, _ = grad_ref.shape
    rows = size // 2
    position, tile = lax.axis_index("pos"), lax.axis_index("tile")
    parity = lax.rem(position, 2)
    half = rows // 2
    spread[:, :, :rows] = jnp.zeros(spread.shape[:2] + (rows, size), F32)
    spread[:, :, rows + size :] = jnp.zeros(spread.shape[:2] + (rows + 8, size), F32)
    spread[:, :, rows : rows + size] = grad_ref[...]
    for place, strip in enumerate((2 * (1 - parity), 2 * parity, 1)):
        for part in (0, 1):
            for ref, which in ((keep_ref, tile), (send_ref, 1 - tile)):
                total = None
                for slot in range(slots):
                    start = offset_ref[slot, 0] - (position - 1) * rows
                    begin = rows - start + strip * rows + which * half
                    value = load_rows(spread, (slot, part), begin, half)
                    total = value if total is None else total + value
                ref[place, part] = total


def finish_kernel(counts, probe_ref, strip_ref, mid_ref, pair_ref, next_ref, *refs):
    object_ref, out_ref = refs[-2:]
    half = object_ref.shape[1]
    begin = pl.multiple_of(lax.axis_index("tile") * half, half)
    object_ref[...] = strip_ref[:, pl.ds(begin, half), :] + object_step * (
        mid_ref[...] + pair_ref[...] + next_ref[...]
    )
    modes = sum(group for group, _ in counts)
    mode = 0
    for group, terms in counts:
        group_refs, refs = refs[:terms], refs[terms:]
        for index in range(group):
            for part in range(out_ref.shape[0]):
                value = sum(ref[index, part] for ref in group_refs)
                rows, columns = value.shape
                lines = columns // 128
                for line in range(lines):
                    where = pl.ds(line * modes + mode, rows, stride=lines * modes)
                    out_ref[part, where, :] = probe_ref[part, where, :] + probe_step * (
                        value[:, line * 128 : (line + 1) * 128]
                    )
            mode += 1


def call(kernel, out_shape, scalars, arrays, name, **options):
    smem = pl.BlockSpec(memory_space=pltpu.SMEM)
    vmem = pl.BlockSpec(memory_space=pltpu.VMEM)
    return pl.pallas_call(
        kernel,
        out_shape=out_shape,
        in_specs=[smem] * len(scalars) + [vmem] * len(arrays),
        out_specs=(vmem,) * len(out_shape),
        compiler_params=pltpu.CompilerParams(vmem_limit_bytes=VMEM_LIMIT),
        cost_estimate=pl.CostEstimate(flops=COSTS[name], bytes_accessed=0, transcendentals=0),
        name=name,
        **options,
    )(*scalars, *arrays)


def shape(*sizes):
    return jax.ShapeDtypeStruct(sizes, F32)


def on_device(object_field, probe, measured, offsets, counts):
    parts, strip_rows, columns = object_field.shape
    slots, size, _ = measured.shape
    modes = probe.shape[1]
    half = size // 2
    positions = lax.axis_size("pos")
    tiles = lax.axis_size("tile")
    position = lax.axis_index("pos")
    tile = lax.axis_index("tile")
    swap = [(0, 1), (1, 0)]
    pair = [(i, i ^ 1) for i in range(positions)]
    following = [(i, i + 1) for i in range(1, positions - 1, 2)]
    following += [(target, source) for source, target in following]
    tables = [jnp.asarray(table) for table in real_tables(size)]
    scratch = [
        pltpu.VMEM((2, size, 3 * size), BF16),
        pltpu.VMEM((2, 3 * size, size), BF16),
        pltpu.VMEM((2, size, size), F32),
    ]

    component = lax.dynamic_index_in_dim(object_field, tile, 0, keepdims=False)
    halo = [lax.ppermute(component, "pos", ring) for ring in (pair, following)]

    pixel_lines = size * size // 128
    share = pixel_lines // positions * modes
    order = np.zeros((size, size), ml_dtypes.bfloat16)
    for parity in (0, 1):
        for index in range(half):
            order[2 * index + parity, parity * half + index] = 1
    probe_lines = probe.reshape(parts, modes, pixel_lines, 128).transpose(0, 2, 1, 3)
    probe_grid, probe_own = call(
        prepare_kernel,
        (shape(parts, modes, size, size), shape(parts, share, 128)),
        [],
        [probe_lines.reshape(parts, pixel_lines * modes, 128)],
        "prepare",
    )
    (amplitude,) = call(
        order_kernel,
        (shape(slots, 2, half, size),),
        [],
        [measured, jnp.asarray(np.stack([order, order.T]))],
        "order",
    )
    from_pair, probe_grid = lax.optimization_barrier((halo[0], probe_grid))
    pair_other = lax.ppermute(from_pair, "tile", swap)
    from_next, pair_other = lax.optimization_barrier((halo[1], pair_other))
    halo = [from_pair, from_next, pair_other, lax.ppermute(from_next, "tile", swap)]

    far, power, patch = [], [], []
    for slot in range(slots):
        outs = call(
            functools.partial(forward_kernel, slot),
            (shape(modes, 2, size, size), shape(2, half, size), shape(parts, size, size)),
            [],
            [offsets, object_field, *halo, probe_grid, *tables],
            "forward",
            scratch_shapes=[pltpu.VMEM((parts, 3 * strip_rows + 8, columns), F32)] + scratch,
        )
        far.append(outs[0])
        power.append(outs[1])
        patch.append(outs[2])
    others = [lax.ppermute(value, "tile", swap) for value in power]

    block_rows = size // positions
    bit_count = positions.bit_length() - 1
    pending = []
    begin = 0
    for group, bits in GROUPS:
        bits = [*bits, *range(len(bits), bit_count)]
        first = begin == 0
        kernel = functools.partial(
            inverse_kernel, tuple(range(begin, begin + group)), bits, first, slots
        )
        outs = (shape(slots, 2, size, size), shape(positions, group, 2, block_rows, size))
        arrays = [*tables, probe_grid, *far, *patch]
        if first:
            outs += (shape(slots, 2, half, size),)
            arrays += [amplitude, *power, *others]
            grad, blocks, ratio = call(
                kernel, outs, [counts], arrays, "inverse", scratch_shapes=scratch
            )
        else:
            arrays += [grad, ratio]
            grad, blocks = call(
                kernel,
                outs,
                [],
                arrays,
                "inverse",
                input_output_aliases={len(arrays) - 2: 0},
                scratch_shapes=scratch,
            )
        begin += group
        pending.append((bits, blocks))

    half_rows = strip_rows // tiles
    strip_shape = shape(3, parts, half_rows, columns)
    kept, sent = call(
        strip_kernel,
        (strip_shape, strip_shape),
        [],
        [offsets, grad],
        "strips",
        scratch_shapes=[pltpu.VMEM((slots, parts, 2 * strip_rows + size + 8, columns), F32)],
    )
    strips = kept + lax.ppermute(sent, "tile", swap)
    from_pair = lax.ppermute(strips[0], "pos", pair)
    from_next = lax.ppermute(strips[1], "pos", following)

    sums = []
    for which, (bits, blocks) in enumerate(pending):
        for step, bit in enumerate(bits):
            if TIE and (which, step) == TIE:
                blocks, from_pair, from_next = lax.optimization_barrier(
                    (blocks, from_pair, from_next)
                )
            keep, send = jnp.split(blocks, 2)
            got = lax.ppermute(send, "pos", [(i, i ^ 2**bit) for i in range(positions)])
            blocks = keep + got
        sums.append([keep[0], got[0]])

    object_out, probe_out = call(
        functools.partial(finish_kernel, [(group, 2) for group, _ in GROUPS]),
        (shape(parts, half_rows, columns), shape(parts, share, 128)),
        [],
        [probe_own, object_field, strips[2], from_pair, from_next, *sum(sums, [])],
        "finish",
    )
    probe_out = probe_out.reshape(parts, share // modes, modes, 128).transpose(0, 2, 1, 3)
    return (object_out, probe_out.reshape(parts, modes, share // modes * 128))


def solution(mesh):
    in_specs = (
        P(None, ("group", "pos"), None),
        P(None, "tile", None),
        P(("group", "pos"), None, None),
        P(("group", "pos"), None),
        P(("group", "pos")),
    )
    out_specs = (P(None, ("group", "pos", "tile"), None), P(None, ("group", "tile"), "pos"))
    return jax.shard_map(
        on_device, mesh=mesh, in_specs=in_specs, out_specs=out_specs, check_vma=False
    )
```

```python
import functools
import math

import jax
import jax.numpy as jnp
import ml_dtypes
import numpy as np
from jax import lax
from jax.experimental import pallas as pl
from jax.experimental.pallas import tpu as pltpu
from jax.sharding import PartitionSpec as P

damping_factor = 0.1
object_step = 0.5
probe_step = 0.05

F32 = jnp.float32
BF16 = jnp.bfloat16
VMEM_LIMIT = 16 * 1024 * 1024
COSTS = {'prepare': 2000000000, 'forward': 4000000000, 'inverse': 2400000000, 'strips': 1200000000, 'finish': 1000000000, 'order': 1000000000, 'pick': 1000000}
CHUNK = 64
TIE = None
GROUPS = ((1, (1, 0, 2)), (1, (0, 1, 2)), (1, (1, 0, 2)), (1, (0, 1, 2)))


def real_tables(size):
    half = size // 2
    counter = np.arange(half)
    phase = np.outer(counter, counter) % half
    even = np.exp(-2j * np.pi * phase / half) / math.sqrt(size)
    odd = even * np.exp(-2j * np.pi * counter / size)[:, None]
    right, left = [], []
    for matrix in (even, odd):
        real = np.block([[matrix.real, matrix.imag], [-matrix.imag, matrix.real]])
        for form in (real, real.T):
            high = form.astype(ml_dtypes.bfloat16)
            low = (form - high.astype(np.float64)).astype(ml_dtypes.bfloat16)
            right.append(np.concatenate([high, high, low], 0))
            left.append(np.concatenate([high, high, low], 1))
    return np.stack(right), np.stack(left)


def split(value):
    high = value.astype(BF16)
    return high, (value - high.astype(F32)).astype(BF16)


def product(left, right):
    return jnp.dot(left, right, preferred_element_type=F32)


def put_left(ref, parity, begin, value):
    size = value.shape[1]
    lines = slice(begin, begin + value.shape[0])
    high, low = split(value)
    ref[parity, lines, :size] = high
    ref[parity, lines, size : 2 * size] = low
    ref[parity, lines, 2 * size :] = high


def put_right(ref, parity, begin, value):
    size = value.shape[1]
    high, low = split(value)
    for index, piece in enumerate((high, low, high)):
        ref[parity, index * size + begin : index * size + begin + value.shape[0]] = piece


def spans(size, count):
    return [(begin, slice(begin, begin + count)) for begin in range(0, size, count)]


def pieces_of(value):
    high, middle = split(value)
    low = (value - high.astype(F32) - middle.astype(F32)).astype(BF16)
    return high, middle, low


def prepare_kernel(probe_ref, grid_ref, own_ref):
    parts, modes, size, columns = grid_ref.shape
    lines = columns // 128
    for part in range(parts):
        for mode in range(modes):
            for line in range(lines):
                grid_ref[part, mode, :, line * 128 : (line + 1) * 128] = probe_ref[
                    part, pl.ds(line * modes + mode, size, stride=lines * modes), :
                ]
    share = own_ref.shape[1]
    own_ref[...] = probe_ref[:, pl.ds(pl.multiple_of(lax.axis_index("pos") * share, share), share), :]


def order_kernel(measured_ref, order_ref, out_ref):
    half = order_ref.shape[1] // 2
    columns, rows = order_ref[0], order_ref[1]
    for slot in range(measured_ref.shape[0]):
        value = jnp.sqrt(measured_ref[slot] + damping_factor)
        value = sum(product(piece, columns) for piece in pieces_of(value))
        value = sum(product(rows, piece) for piece in pieces_of(value))
        out_ref[slot, 0] = value[:half]
        out_ref[slot, 1] = value[half:]


def load_rows(ref, index, begin, count):
    offset = lax.rem(begin, 8)
    span = count + 8
    value = ref[(*index, pl.ds(pl.multiple_of(begin - offset, 8), span))]
    return pltpu.roll(value, lax.rem(span - offset, span), 0)[:count]


def forward_kernel(
    slot, offset_ref, own_ref, pair_ref, next_ref, pair_other_ref, next_other_ref,
    probe_ref, row_ref, col_ref, far_ref, power_ref, patch_ref, extended, left_ref, right_ref,
    middle_ref,
):
    rows = own_ref.shape[1]
    size = patch_ref.shape[1]
    position, tile = lax.axis_index("pos"), lax.axis_index("tile")
    parity = lax.rem(position, 2)
    start = offset_ref[slot, 0] - (position - 1) * rows
    extended[:, rows : 2 * rows] = own_ref[...]
    for side, mine, other in (
        (1 - parity, pair_ref, pair_other_ref),
        (parity, next_ref, next_other_ref),
    ):
        lines = pl.ds(pl.multiple_of(side * (2 * rows), rows), rows)
        extended[tile, lines] = mine[...]
        extended[1 - tile, lines] = other[...]
    for part in (0, 1):
        patch_ref[part] = load_rows(extended, (part,), start, size)
    half = size // 2
    modes = probe_ref.shape[1]

    def spread_rows(mode):
        for begin, lines in spans(size, CHUNK):
            patch_real, patch_imag = patch_ref[0, lines], patch_ref[1, lines]
            probe_real, probe_imag = probe_ref[0, mode, lines], probe_ref[1, mode, lines]
            real = probe_real * patch_real - probe_imag * patch_imag
            imag = probe_real * patch_imag + probe_imag * patch_real
            a, b = real[:, :half], real[:, half:]
            c, d = imag[:, :half], imag[:, half:]
            put_left(left_ref, 2 * (mode % 2), begin, jnp.concatenate([a + b, c + d], 1))
            put_left(left_ref, 2 * (mode % 2) + 1, begin, jnp.concatenate([a - b, c - d], 1))

    def row_products(mode):
        for parity in (0, 1):
            which = 2 * (mode % 2) + parity
            middle_ref[which] = product(left_ref[which], row_ref[2 * parity])

    def spread_columns(mode):
        first = 2 * (mode % 2)
        for begin, lines in spans(half, CHUNK // 2):
            under = slice(half + begin, half + begin + CHUNK // 2)
            for part in (0, 1):
                where = slice(part * half, (part + 1) * half)
                top = jnp.concatenate(
                    [middle_ref[first, lines, where], middle_ref[first + 1, lines, where]], 1
                )
                low = jnp.concatenate(
                    [middle_ref[first, under, where], middle_ref[first + 1, under, where]], 1
                )
                put_right(right_ref, first, part * half + begin, top + low)
                put_right(right_ref, first + 1, part * half + begin, top - low)

    def column_products(mode):
        for parity in (0, 1):
            which = 2 * (mode % 2) + parity
            far_ref[mode, parity] = product(col_ref[2 * parity + 1], right_ref[which])

    def add_power(mode):
        for parity in (0, 1):
            for begin, lines in spans(half, CHUNK):
                under = slice(half + begin, half + begin + CHUNK)
                real, imag = far_ref[mode, parity, lines], far_ref[mode, parity, under]
                power = real * real + imag * imag
                if mode == 0:
                    power_ref[parity, lines] = power
                else:
                    power_ref[parity, lines] += power

    spread_rows(0)
    row_products(0)
    for mode in range(modes):
        if mode + 1 < modes:
            spread_rows(mode + 1)
        spread_columns(mode)
        if mode + 1 < modes:
            row_products(mode + 1)
        column_products(mode)
        if mode > 0:
            add_power(mode - 1)
    add_power(modes - 1)


def block_index(block, position, bits):
    index = 0
    for bit in bits:
        differs = lax.rem(lax.div(position, 2**bit) + (block >> bit) % 2, 2)
        index = 2 * index + differs
    return index


def inverse_kernel(modes, bits, first, slots, *refs):
    if first:
        count_ref, *refs = refs
    row_ref, col_ref, probe_ref, *refs = refs
    *refs, left_ref, right_ref, middle_ref = refs
    far_refs, patch_refs = refs[:slots], refs[slots : 2 * slots]
    refs = refs[2 * slots :]
    if first:
        amplitude_ref, power_refs = refs[0], refs[1 : 1 + slots]
        other_refs = refs[1 + slots : 1 + 2 * slots]
        grad_ref, block_ref, ratio_ref = refs[1 + 2 * slots :]
        for slot in range(slots):
            model = jnp.sqrt(power_refs[slot][...] + other_refs[slot][...] + damping_factor)
            active = (slot < count_ref[0]).astype(F32)
            ratio_ref[slot] = (amplitude_ref[slot] / model - 1.0) * active
    else:
        _, ratio_ref, grad_ref, block_ref = refs
    size = probe_ref.shape[2]
    blocks, rows = block_ref.shape[0], block_ref.shape[3]
    half = size // 2
    position = lax.axis_index("pos")

    def spread_columns(slot, mode, parity):
        for begin, lines in spans(half, CHUNK):
            under = slice(half + begin, half + begin + CHUNK)
            ratio = ratio_ref[slot, parity, lines]
            far = far_refs[slot].at[mode, parity]
            put_right(right_ref, 2 * slot + parity, begin, far[lines] * ratio)
            put_right(right_ref, 2 * slot + parity, half + begin, far[under] * ratio)

    def column_products(slot, parity):
        which = 2 * slot + parity
        middle_ref[which] = product(col_ref[2 * parity], right_ref[which])

    def spread_rows(slot):
        for begin, lines in spans(half, CHUNK // 2):
            under = slice(half + begin, half + begin + CHUNK // 2)
            for offset, sign in ((0, 1.0), (half, -1.0)):
                real = middle_ref[2 * slot, lines] + sign * middle_ref[2 * slot + 1, lines]
                imag = middle_ref[2 * slot, under] + sign * middle_ref[2 * slot + 1, under]
                for parity in (0, 1):
                    where = slice(parity * half, (parity + 1) * half)
                    value = jnp.concatenate([real[:, where], imag[:, where]], 1)
                    put_left(left_ref, 2 * slot + parity, offset + begin, value)

    def row_products(slot, parity):
        which = 2 * slot + parity
        middle_ref[which] = product(left_ref[which], row_ref[2 * parity + 1])

    def add_terms(slot, index, mode):
        for begin, lines in spans(size, rows):
            target = block_index(begin // rows, position, bits)
            a, b = middle_ref[2 * slot, lines], middle_ref[2 * slot + 1, lines]
            plus, minus = a + b, a - b
            real = jnp.concatenate([plus[:, :half], minus[:, :half]], 1)
            imag = jnp.concatenate([plus[:, half:], minus[:, half:]], 1)
            probe_real, probe_imag = probe_ref[0, mode, lines], probe_ref[1, mode, lines]
            patch_real, patch_imag = patch_refs[slot][0, lines], patch_refs[slot][1, lines]
            grads = (
                probe_real * real + probe_imag * imag,
                probe_real * imag - probe_imag * real,
            )
            terms = (
                patch_real * real + patch_imag * imag,
                patch_real * imag - patch_imag * real,
            )
            for part in (0, 1):
                if first and index == 0:
                    grad_ref[slot, part, lines] = grads[part]
                else:
                    grad_ref[slot, part, lines] += grads[part]
                if slot == 0:
                    block_ref[target, index, part] = terms[part]
                else:
                    block_ref[target, index, part] += terms[part]

    for index, mode in enumerate(modes):
        for slot in range(slots):
            for parity in (0, 1):
                spread_columns(slot, mode, parity)
                column_products(slot, parity)
        for slot in range(slots):
            spread_rows(slot)
            if slot > 0:
                add_terms(slot - 1, index, mode)
            for parity in (0, 1):
                row_products(slot, parity)
        add_terms(slots - 1, index, mode)

def strip_kernel(offset_ref, grad_ref, keep_ref, send_ref, spread):
    slots, _, size, _ = grad_ref.shape
    rows = size // 2
    position, tile = lax.axis_index("pos"), lax.axis_index("tile")
    parity = lax.rem(position, 2)
    half = rows // 2
    spread[:, :, :rows] = jnp.zeros(spread.shape[:2] + (rows, size), F32)
    spread[:, :, rows + size :] = jnp.zeros(spread.shape[:2] + (rows + 8, size), F32)
    spread[:, :, rows : rows + size] = grad_ref[...]
    for place, strip in enumerate((2 * (1 - parity), 2 * parity, 1)):
        for part in (0, 1):
            for ref, which in ((keep_ref, tile), (send_ref, 1 - tile)):
                total = None
                for slot in range(slots):
                    start = offset_ref[slot, 0] - (position - 1) * rows
                    begin = rows - start + strip * rows + which * half
                    value = load_rows(spread, (slot, part), begin, half)
                    total = value if total is None else total + value
                ref[place, part] = total


def finish_kernel(counts, probe_ref, strip_ref, mid_ref, pair_ref, next_ref, *refs):
    object_ref, out_ref = refs[-2:]
    half = object_ref.shape[1]
    begin = pl.multiple_of(lax.axis_index("tile") * half, half)
    object_ref[...] = strip_ref[:, pl.ds(begin, half), :] + object_step * (
        mid_ref[...] + pair_ref[...] + next_ref[...]
    )
    modes = sum(group for group, _ in counts)
    mode = 0
    for group, terms in counts:
        group_refs, refs = refs[:terms], refs[terms:]
        for index in range(group):
            for part in range(out_ref.shape[0]):
                value = sum(ref[index, part] for ref in group_refs)
                rows, columns = value.shape
                lines = columns // 128
                for line in range(lines):
                    where = pl.ds(line * modes + mode, rows, stride=lines * modes)
                    out_ref[part, where, :] = probe_ref[part, where, :] + probe_step * (
                        value[:, line * 128 : (line + 1) * 128]
                    )
            mode += 1


def pick_kernel(part_ref, out_ref):
    out_ref[...] = part_ref[...]


def call(kernel, out_shape, scalars, arrays, name, **options):
    smem = pl.BlockSpec(memory_space=pltpu.SMEM)
    vmem = pl.BlockSpec(memory_space=pltpu.VMEM)
    return pl.pallas_call(
        kernel,
        out_shape=out_shape,
        in_specs=[smem] * len(scalars) + [vmem] * len(arrays),
        out_specs=(vmem,) * len(out_shape),
        compiler_params=pltpu.CompilerParams(vmem_limit_bytes=VMEM_LIMIT),
        cost_estimate=pl.CostEstimate(flops=COSTS[name], bytes_accessed=0, transcendentals=0),
        name=name,
        **options,
    )(*scalars, *arrays)


def shape(*sizes):
    return jax.ShapeDtypeStruct(sizes, F32)


def on_device(object_field, probe, measured, offsets, counts):
    parts, strip_rows, columns = object_field.shape
    slots, size, _ = measured.shape
    modes = probe.shape[1]
    half = size // 2
    positions = lax.axis_size("pos")
    tiles = lax.axis_size("tile")
    position = lax.axis_index("pos")
    tile = lax.axis_index("tile")
    swap = [(0, 1), (1, 0)]
    pair = [(i, i ^ 1) for i in range(positions)]
    following = [(i, i + 1) for i in range(1, positions - 1, 2)]
    following += [(target, source) for source, target in following]
    tables = [jnp.asarray(table) for table in real_tables(size)]
    scratch = [
        pltpu.VMEM((4, size, 3 * size), BF16),
        pltpu.VMEM((4, 3 * size, size), BF16),
        pltpu.VMEM((4, size, size), F32),
    ]

    component = lax.dynamic_index_in_dim(object_field, tile, 0, keepdims=False)
    from_pair = lax.ppermute(component, "pos", pair)

    pixel_lines = size * size // 128
    share = pixel_lines // positions * modes
    order = np.zeros((size, size), ml_dtypes.bfloat16)
    for parity in (0, 1):
        for index in range(half):
            order[2 * index + parity, parity * half + index] = 1
    probe_lines = probe.reshape(parts, modes, pixel_lines, 128).transpose(0, 2, 1, 3)
    probe_grid, probe_own = call(
        prepare_kernel,
        (shape(parts, modes, size, size), shape(parts, share, 128)),
        [],
        [probe_lines.reshape(parts, pixel_lines * modes, 128)],
        "prepare",
    )
    (amplitude,) = call(
        order_kernel,
        (shape(slots, 2, half, size),),
        [],
        [measured, jnp.asarray(np.stack([order, order.T]))],
        "order",
    )
    (again,) = call(pick_kernel, (shape(strip_rows, columns),), [], [component], "pick")
    from_next = lax.ppermute(again, "pos", following)
    from_pair, probe_grid = lax.optimization_barrier((from_pair, probe_grid))
    pair_other = lax.ppermute(from_pair, "tile", swap)
    from_next, pair_other = lax.optimization_barrier((from_next, pair_other))
    halo = [from_pair, from_next, pair_other, lax.ppermute(from_next, "tile", swap)]

    far, power, patch = [], [], []
    for slot in range(slots):
        outs = call(
            functools.partial(forward_kernel, slot),
            (shape(modes, 2, size, size), shape(2, half, size), shape(parts, size, size)),
            [],
            [offsets, object_field, *halo, probe_grid, *tables],
            "forward",
            scratch_shapes=[pltpu.VMEM((parts, 3 * strip_rows + 8, columns), F32)] + scratch,
        )
        far.append(outs[0])
        power.append(outs[1])
        patch.append(outs[2])
    others = [lax.ppermute(value, "tile", swap) for value in power]

    block_rows = size // positions
    bit_count = positions.bit_length() - 1
    pending = []
    begin = 0
    for group, bits in GROUPS:
        bits = [*bits, *range(len(bits), bit_count)]
        first = begin == 0
        kernel = functools.partial(
            inverse_kernel, tuple(range(begin, begin + group)), bits, first, slots
        )
        outs = (shape(slots, 2, size, size), shape(positions, group, 2, block_rows, size))
        arrays = [*tables, probe_grid, *far, *patch]
        if first:
            outs += (shape(slots, 2, half, size),)
            arrays += [amplitude, *power, *others]
            grad, blocks, ratio = call(
                kernel, outs, [counts], arrays, "inverse", scratch_shapes=scratch
            )
        else:
            arrays += [grad, ratio]
            grad, blocks = call(
                kernel,
                outs,
                [],
                arrays,
                "inverse",
                input_output_aliases={len(arrays) - 2: 0},
                scratch_shapes=scratch,
            )
        begin += group
        pending.append((bits, blocks))

    half_rows = strip_rows // tiles
    strip_shape = shape(3, parts, half_rows, columns)
    kept, sent = call(
        strip_kernel,
        (strip_shape, strip_shape),
        [],
        [offsets, grad],
        "strips",
        scratch_shapes=[pltpu.VMEM((slots, parts, 2 * strip_rows + size + 8, columns), F32)],
    )
    strips = kept + lax.ppermute(sent, "tile", swap)
    from_pair = lax.ppermute(strips[0], "pos", pair)
    from_next = lax.ppermute(strips[1], "pos", following)

    sums = []
    for which, (bits, blocks) in enumerate(pending):
        for step, bit in enumerate(bits):
            if TIE and (which, step) == TIE:
                blocks, from_pair, from_next = lax.optimization_barrier(
                    (blocks, from_pair, from_next)
                )
            keep, send = jnp.split(blocks, 2)
            got = lax.ppermute(send, "pos", [(i, i ^ 2**bit) for i in range(positions)])
            blocks = keep + got
        sums.append([keep[0], got[0]])

    object_out, probe_out = call(
        functools.partial(finish_kernel, [(group, 2) for group, _ in GROUPS]),
        (shape(parts, half_rows, columns), shape(parts, share, 128)),
        [],
        [probe_own, object_field, strips[2], from_pair, from_next, *sum(sums, [])],
        "finish",
    )
    probe_out = probe_out.reshape(parts, share // modes, modes, 128).transpose(0, 2, 1, 3)
    return (object_out, probe_out.reshape(parts, modes, share // modes * 128))


def solution(mesh):
    in_specs = (
        P(None, ("group", "pos"), None),
        P(None, "tile", None),
        P(("group", "pos"), None, None),
        P(("group", "pos"), None),
        P(("group", "pos")),
    )
    out_specs = (P(None, ("group", "pos", "tile"), None), P(None, ("group", "tile"), "pos"))
    return jax.shard_map(
        on_device, mesh=mesh, in_specs=in_specs, out_specs=out_specs, check_vma=False
    )
```

```python
import functools
import math

import jax
import jax.numpy as jnp
import ml_dtypes
import numpy as np
from jax import lax
from jax.experimental import pallas as pl
from jax.experimental.pallas import tpu as pltpu
from jax.sharding import PartitionSpec as P

damping_factor = 0.1
object_step = 0.5
probe_step = 0.05

F32 = jnp.float32
BF16 = jnp.bfloat16
VMEM_LIMIT = 16 * 1024 * 1024
COSTS = {'prepare': 2000000000, 'forward': 4000000000, 'inverse': 2400000000, 'strips': 1200000000, 'finish': 1000000000, 'order': 1000000000, 'pick': 1000000}
CHUNK = 64
PATTERN = (0, 1, 0, 1)
STEPS = (((0,), 1), ((1,), 0), ((2,), 1), ((3,), 0), ((0,), 0), ((1,), 1), ((2,), 0), ((3,), 1), ((0, 1), 2), ((2, 3), 2))


def real_tables(size):
    half = size // 2
    counter = np.arange(half)
    phase = np.outer(counter, counter) % half
    even = np.exp(-2j * np.pi * phase / half) / math.sqrt(size)
    odd = even * np.exp(-2j * np.pi * counter / size)[:, None]
    right, left = [], []
    for matrix in (even, odd):
        real = np.block([[matrix.real, matrix.imag], [-matrix.imag, matrix.real]])
        for form in (real, real.T):
            high = form.astype(ml_dtypes.bfloat16)
            low = (form - high.astype(np.float64)).astype(ml_dtypes.bfloat16)
            right.append(np.concatenate([high, high, low], 0))
            left.append(np.concatenate([high, high, low], 1))
    return np.stack(right), np.stack(left)


def split(value):
    high = value.astype(BF16)
    return high, (value - high.astype(F32)).astype(BF16)


def product(left, right):
    return jnp.dot(left, right, preferred_element_type=F32)


def put_left(ref, parity, begin, value):
    size = value.shape[1]
    lines = slice(begin, begin + value.shape[0])
    high, low = split(value)
    ref[parity, lines, :size] = high
    ref[parity, lines, size : 2 * size] = low
    ref[parity, lines, 2 * size :] = high


def put_right(ref, parity, begin, value):
    size = value.shape[1]
    high, low = split(value)
    for index, piece in enumerate((high, low, high)):
        ref[parity, index * size + begin : index * size + begin + value.shape[0]] = piece


def spans(size, count):
    return [(begin, slice(begin, begin + count)) for begin in range(0, size, count)]


def pieces_of(value):
    high, middle = split(value)
    low = (value - high.astype(F32) - middle.astype(F32)).astype(BF16)
    return high, middle, low


def prepare_kernel(probe_ref, grid_ref, own_ref):
    parts, modes, size, columns = grid_ref.shape
    lines = columns // 128
    for part in range(parts):
        for mode in range(modes):
            for line in range(lines):
                grid_ref[part, mode, :, line * 128 : (line + 1) * 128] = probe_ref[
                    part, pl.ds(line * modes + mode, size, stride=lines * modes), :
                ]
    share = own_ref.shape[1]
    own_ref[...] = probe_ref[:, pl.ds(pl.multiple_of(lax.axis_index("pos") * share, share), share), :]


def order_kernel(measured_ref, order_ref, out_ref):
    half = order_ref.shape[1] // 2
    columns, rows = order_ref[0], order_ref[1]
    for slot in range(measured_ref.shape[0]):
        value = jnp.sqrt(measured_ref[slot] + damping_factor)
        value = sum(product(piece, columns) for piece in pieces_of(value))
        value = sum(product(rows, piece) for piece in pieces_of(value))
        out_ref[slot, 0] = value[:half]
        out_ref[slot, 1] = value[half:]


def load_rows(ref, index, begin, count):
    offset = lax.rem(begin, 8)
    span = count + 8
    value = ref[(*index, pl.ds(pl.multiple_of(begin - offset, 8), span))]
    return pltpu.roll(value, lax.rem(span - offset, span), 0)[:count]


def forward_kernel(
    slot, offset_ref, own_ref, pair_ref, next_ref, pair_other_ref, next_other_ref,
    probe_ref, row_ref, col_ref, far_ref, power_ref, patch_ref, extended, left_ref, right_ref,
    middle_ref,
):
    rows = own_ref.shape[1]
    size = patch_ref.shape[1]
    position, tile = lax.axis_index("pos"), lax.axis_index("tile")
    parity = lax.rem(position, 2)
    start = offset_ref[slot, 0] - (position - 1) * rows
    extended[:, rows : 2 * rows] = own_ref[...]
    for side, mine, other in (
        (1 - parity, pair_ref, pair_other_ref),
        (parity, next_ref, next_other_ref),
    ):
        lines = pl.ds(pl.multiple_of(side * (2 * rows), rows), rows)
        extended[tile, lines] = mine[...]
        extended[1 - tile, lines] = other[...]
    for part in (0, 1):
        patch_ref[part] = load_rows(extended, (part,), start, size)
    half = size // 2
    modes = probe_ref.shape[1]

    def spread_rows(mode):
        for begin, lines in spans(size, CHUNK):
            patch_real, patch_imag = patch_ref[0, lines], patch_ref[1, lines]
            probe_real, probe_imag = probe_ref[0, mode, lines], probe_ref[1, mode, lines]
            real = probe_real * patch_real - probe_imag * patch_imag
            imag = probe_real * patch_imag + probe_imag * patch_real
            a, b = real[:, :half], real[:, half:]
            c, d = imag[:, :half], imag[:, half:]
            put_left(left_ref, 2 * (mode % 2), begin, jnp.concatenate([a + b, c + d], 1))
            put_left(left_ref, 2 * (mode % 2) + 1, begin, jnp.concatenate([a - b, c - d], 1))

    def row_products(mode):
        for parity in (0, 1):
            which = 2 * (mode % 2) + parity
            middle_ref[which] = product(left_ref[which], row_ref[2 * parity])

    def spread_columns(mode):
        first = 2 * (mode % 2)
        for begin, lines in spans(half, CHUNK // 2):
            under = slice(half + begin, half + begin + CHUNK // 2)
            for part in (0, 1):
                where = slice(part * half, (part + 1) * half)
                top = jnp.concatenate(
                    [middle_ref[first, lines, where], middle_ref[first + 1, lines, where]], 1
                )
                low = jnp.concatenate(
                    [middle_ref[first, under, where], middle_ref[first + 1, under, where]], 1
                )
                put_right(right_ref, first, part * half + begin, top + low)
                put_right(right_ref, first + 1, part * half + begin, top - low)

    def column_products(mode):
        for parity in (0, 1):
            which = 2 * (mode % 2) + parity
            far_ref[mode, parity] = product(col_ref[2 * parity + 1], right_ref[which])

    def add_power(mode):
        for parity in (0, 1):
            for begin, lines in spans(half, CHUNK):
                under = slice(half + begin, half + begin + CHUNK)
                real, imag = far_ref[mode, parity, lines], far_ref[mode, parity, under]
                power = real * real + imag * imag
                if mode == 0:
                    power_ref[parity, lines] = power
                else:
                    power_ref[parity, lines] += power

    spread_rows(0)
    row_products(0)
    for mode in range(modes):
        if mode + 1 < modes:
            spread_rows(mode + 1)
        spread_columns(mode)
        if mode + 1 < modes:
            row_products(mode + 1)
        column_products(mode)
        if mode > 0:
            add_power(mode - 1)
    add_power(modes - 1)


def block_index(block, position, bits):
    index = 0
    for bit in bits:
        differs = lax.rem(lax.div(position, 2**bit) + (block >> bit) % 2, 2)
        index = 2 * index + differs
    return index


def inverse_kernel(modes, bits, first, slots, *refs):
    if first:
        count_ref, *refs = refs
    row_ref, col_ref, probe_ref, *refs = refs
    *refs, left_ref, right_ref, middle_ref = refs
    far_refs, patch_refs = refs[:slots], refs[slots : 2 * slots]
    refs = refs[2 * slots :]
    if first:
        amplitude_ref, power_refs = refs[0], refs[1 : 1 + slots]
        other_refs = refs[1 + slots : 1 + 2 * slots]
        grad_ref, block_ref, ratio_ref = refs[1 + 2 * slots :]
        for slot in range(slots):
            model = jnp.sqrt(power_refs[slot][...] + other_refs[slot][...] + damping_factor)
            active = (slot < count_ref[0]).astype(F32)
            ratio_ref[slot] = (amplitude_ref[slot] / model - 1.0) * active
    else:
        _, ratio_ref, grad_ref, block_ref = refs
    size = probe_ref.shape[2]
    blocks, rows = block_ref.shape[0], block_ref.shape[3]
    half = size // 2
    position = lax.axis_index("pos")

    def spread_columns(slot, mode, parity):
        for begin, lines in spans(half, CHUNK):
            under = slice(half + begin, half + begin + CHUNK)
            ratio = ratio_ref[slot, parity, lines]
            far = far_refs[slot].at[mode, parity]
            put_right(right_ref, 2 * slot + parity, begin, far[lines] * ratio)
            put_right(right_ref, 2 * slot + parity, half + begin, far[under] * ratio)

    def column_products(slot, parity):
        which = 2 * slot + parity
        middle_ref[which] = product(col_ref[2 * parity], right_ref[which])

    def spread_rows(slot):
        for begin, lines in spans(half, CHUNK // 2):
            under = slice(half + begin, half + begin + CHUNK // 2)
            for offset, sign in ((0, 1.0), (half, -1.0)):
                real = middle_ref[2 * slot, lines] + sign * middle_ref[2 * slot + 1, lines]
                imag = middle_ref[2 * slot, under] + sign * middle_ref[2 * slot + 1, under]
                for parity in (0, 1):
                    where = slice(parity * half, (parity + 1) * half)
                    value = jnp.concatenate([real[:, where], imag[:, where]], 1)
                    put_left(left_ref, 2 * slot + parity, offset + begin, value)

    def row_products(slot, parity):
        which = 2 * slot + parity
        middle_ref[which] = product(left_ref[which], row_ref[2 * parity + 1])

    def add_terms(slot, index, mode):
        for begin, lines in spans(size, rows):
            target = block_index(begin // rows, position, bits)
            a, b = middle_ref[2 * slot, lines], middle_ref[2 * slot + 1, lines]
            plus, minus = a + b, a - b
            real = jnp.concatenate([plus[:, :half], minus[:, :half]], 1)
            imag = jnp.concatenate([plus[:, half:], minus[:, half:]], 1)
            probe_real, probe_imag = probe_ref[0, mode, lines], probe_ref[1, mode, lines]
            patch_real, patch_imag = patch_refs[slot][0, lines], patch_refs[slot][1, lines]
            grads = (
                probe_real * real + probe_imag * imag,
                probe_real * imag - probe_imag * real,
            )
            terms = (
                patch_real * real + patch_imag * imag,
                patch_real * imag - patch_imag * real,
            )
            for part in (0, 1):
                if first and index == 0:
                    grad_ref[slot, part, lines] = grads[part]
                else:
                    grad_ref[slot, part, lines] += grads[part]
                if slot == 0:
                    block_ref[target, index, part] = terms[part]
                else:
                    block_ref[target, index, part] += terms[part]

    for index, mode in enumerate(modes):
        for slot in range(slots):
            for parity in (0, 1):
                spread_columns(slot, mode, parity)
                column_products(slot, parity)
        for slot in range(slots):
            spread_rows(slot)
            if slot > 0:
                add_terms(slot - 1, index, mode)
            for parity in (0, 1):
                row_products(slot, parity)
        add_terms(slots - 1, index, mode)

def strip_kernel(offset_ref, grad_ref, keep_ref, send_ref, spread):
    slots, _, size, _ = grad_ref.shape
    rows = size // 2
    position, tile = lax.axis_index("pos"), lax.axis_index("tile")
    parity = lax.rem(position, 2)
    half = rows // 2
    spread[:, :, :rows] = jnp.zeros(spread.shape[:2] + (rows, size), F32)
    spread[:, :, rows + size :] = jnp.zeros(spread.shape[:2] + (rows + 8, size), F32)
    spread[:, :, rows : rows + size] = grad_ref[...]
    for place, strip in enumerate((2 * (1 - parity), 2 * parity, 1)):
        for part in (0, 1):
            for ref, which in ((keep_ref, tile), (send_ref, 1 - tile)):
                total = None
                for slot in range(slots):
                    start = offset_ref[slot, 0] - (position - 1) * rows
                    begin = rows - start + strip * rows + which * half
                    value = load_rows(spread, (slot, part), begin, half)
                    total = value if total is None else total + value
                ref[place, part] = total


def finish_kernel(counts, probe_ref, strip_ref, mid_ref, pair_ref, next_ref, *refs):
    object_ref, out_ref = refs[-2:]
    half = object_ref.shape[1]
    begin = pl.multiple_of(lax.axis_index("tile") * half, half)
    object_ref[...] = strip_ref[:, pl.ds(begin, half), :] + object_step * (
        mid_ref[...] + pair_ref[...] + next_ref[...]
    )
    modes = sum(group for group, _ in counts)
    mode = 0
    for group, terms in counts:
        group_refs, refs = refs[:terms], refs[terms:]
        for index in range(group):
            for part in range(out_ref.shape[0]):
                value = sum(ref[index, part] for ref in group_refs)
                rows, columns = value.shape
                lines = columns // 128
                for line in range(lines):
                    where = pl.ds(line * modes + mode, rows, stride=lines * modes)
                    out_ref[part, where, :] = probe_ref[part, where, :] + probe_step * (
                        value[:, line * 128 : (line + 1) * 128]
                    )
            mode += 1


def pick_kernel(part_ref, out_ref):
    out_ref[...] = part_ref[...]


def call(kernel, out_shape, scalars, arrays, name, **options):
    smem = pl.BlockSpec(memory_space=pltpu.SMEM)
    vmem = pl.BlockSpec(memory_space=pltpu.VMEM)
    return pl.pallas_call(
        kernel,
        out_shape=out_shape,
        in_specs=[smem] * len(scalars) + [vmem] * len(arrays),
        out_specs=(vmem,) * len(out_shape),
        compiler_params=pltpu.CompilerParams(vmem_limit_bytes=VMEM_LIMIT),
        cost_estimate=pl.CostEstimate(flops=COSTS[name], bytes_accessed=0, transcendentals=0),
        name=name,
        **options,
    )(*scalars, *arrays)


def shape(*sizes):
    return jax.ShapeDtypeStruct(sizes, F32)


def on_device(object_field, probe, measured, offsets, counts):
    parts, strip_rows, columns = object_field.shape
    slots, size, _ = measured.shape
    modes = probe.shape[1]
    half = size // 2
    positions = lax.axis_size("pos")
    tiles = lax.axis_size("tile")
    position = lax.axis_index("pos")
    tile = lax.axis_index("tile")
    swap = [(0, 1), (1, 0)]
    pair = [(i, i ^ 1) for i in range(positions)]
    following = [(i, i + 1) for i in range(1, positions - 1, 2)]
    following += [(target, source) for source, target in following]
    tables = [jnp.asarray(table) for table in real_tables(size)]
    scratch = [
        pltpu.VMEM((4, size, 3 * size), BF16),
        pltpu.VMEM((4, 3 * size, size), BF16),
        pltpu.VMEM((4, size, size), F32),
    ]

    component = lax.dynamic_index_in_dim(object_field, tile, 0, keepdims=False)
    from_pair = lax.ppermute(component, "pos", pair)

    pixel_lines = size * size // 128
    share = pixel_lines // positions * modes
    order = np.zeros((size, size), ml_dtypes.bfloat16)
    for parity in (0, 1):
        for index in range(half):
            order[2 * index + parity, parity * half + index] = 1
    probe_lines = probe.reshape(parts, modes, pixel_lines, 128).transpose(0, 2, 1, 3)
    probe_grid, probe_own = call(
        prepare_kernel,
        (shape(parts, modes, size, size), shape(parts, share, 128)),
        [],
        [probe_lines.reshape(parts, pixel_lines * modes, 128)],
        "prepare",
    )
    (amplitude,) = call(
        order_kernel,
        (shape(slots, 2, half, size),),
        [],
        [measured, jnp.asarray(np.stack([order, order.T]))],
        "order",
    )
    (again,) = call(pick_kernel, (shape(strip_rows, columns),), [], [component], "pick")
    from_next = lax.ppermute(again, "pos", following)
    from_pair, probe_grid = lax.optimization_barrier((from_pair, probe_grid))
    pair_other = lax.ppermute(from_pair, "tile", swap)
    from_next, pair_other = lax.optimization_barrier((from_next, pair_other))
    halo = [from_pair, from_next, pair_other, lax.ppermute(from_next, "tile", swap)]

    far, power, patch = [], [], []
    for slot in range(slots):
        outs = call(
            functools.partial(forward_kernel, slot),
            (shape(modes, 2, size, size), shape(2, half, size), shape(parts, size, size)),
            [],
            [offsets, object_field, *halo, probe_grid, *tables],
            "forward",
            scratch_shapes=[pltpu.VMEM((parts, 3 * strip_rows + 8, columns), F32)] + scratch,
        )
        far.append(outs[0])
        power.append(outs[1])
        patch.append(outs[2])
    others = [lax.ppermute(value, "tile", swap) for value in power]

    block_rows = size // positions
    bit_count = positions.bit_length() - 1
    later = list(range(2, bit_count))
    grad, blocks = None, []
    for mode in range(modes):
        bits = [(1, 0), (0, 1)][PATTERN[mode % 4]]
        kernel = functools.partial(inverse_kernel, (mode,), [*bits, *later], mode == 0, slots)
        outs = (shape(slots, 2, size, size), shape(positions, 1, 2, block_rows, size))
        arrays = [*tables, probe_grid, *far, *patch]
        if mode == 0:
            outs += (shape(slots, 2, half, size),)
            arrays += [amplitude, *power, *others]
            grad, terms, ratio = call(
                kernel, outs, [counts], arrays, "inverse", scratch_shapes=scratch
            )
        else:
            arrays += [grad, ratio]
            grad, terms = call(
                kernel,
                outs,
                [],
                arrays,
                "inverse",
                input_output_aliases={len(arrays) - 2: 0},
                scratch_shapes=scratch,
            )
        blocks.append(jnp.split(terms, 2))

    half_rows = strip_rows // tiles
    strip_shape = shape(3, parts, half_rows, columns)
    kept, sent = call(
        strip_kernel,
        (strip_shape, strip_shape),
        [],
        [offsets, grad],
        "strips",
        scratch_shapes=[pltpu.VMEM((slots, parts, 2 * strip_rows + size + 8, columns), F32)],
    )
    strips = kept + lax.ppermute(sent, "tile", swap)
    def exchange(bit, *sends):
        payload = sends[0] if len(sends) == 1 else jnp.concatenate(sends, 0)
        got = lax.ppermute(payload, "pos", [(i, i ^ 2**bit) for i in range(positions)])
        ends = np.cumsum([send.shape[0] for send in sends])
        return [got[end - send.shape[0] : end] for send, end in zip(sends, ends)]

    def advance(modes_at, bit):
        gots = exchange(bit, *(blocks[mode][1] for mode in modes_at))
        for mode, got in zip(modes_at, gots):
            keep = blocks[mode][0]
            blocks[mode] = jnp.split(keep + got, 2) if keep.shape[0] > 1 else [keep, got]

    for modes_at, bit in STEPS:
        if modes_at == "tie":
            blocks[bit], strips = lax.optimization_barrier((blocks[bit], strips))
            continue
        for now in [bit] if bit < 2 else later:
            advance(modes_at, now)
    from_pair = lax.ppermute(strips[0], "pos", pair)
    from_next = lax.ppermute(strips[1], "pos", following)
    sums = [[keep[0], got[0]] for keep, got in blocks]

    object_out, probe_out = call(
        functools.partial(finish_kernel, [(1, 2)] * modes),
        (shape(parts, half_rows, columns), shape(parts, share, 128)),
        [],
        [probe_own, object_field, strips[2], from_pair, from_next, *sum(sums, [])],
        "finish",
    )
    probe_out = probe_out.reshape(parts, share // modes, modes, 128).transpose(0, 2, 1, 3)
    return (object_out, probe_out.reshape(parts, modes, share // modes * 128))


def solution(mesh):
    in_specs = (
        P(None, ("group", "pos"), None),
        P(None, "tile", None),
        P(("group", "pos"), None, None),
        P(("group", "pos"), None),
        P(("group", "pos")),
    )
    out_specs = (P(None, ("group", "pos", "tile"), None), P(None, ("group", "tile"), "pos"))
    return jax.shard_map(
        on_device, mesh=mesh, in_specs=in_specs, out_specs=out_specs, check_vma=False
    )
```

```python
import functools
import math

import jax
import jax.numpy as jnp
import ml_dtypes
import numpy as np
from jax import lax
from jax.experimental import pallas as pl
from jax.experimental.pallas import tpu as pltpu
from jax.sharding import PartitionSpec as P

damping_factor = 0.1
object_step = 0.5
probe_step = 0.05

F32 = jnp.float32
BF16 = jnp.bfloat16
VMEM_LIMIT = 16 * 1024 * 1024
COSTS = {'prepare': 2000000000, 'forward': 4000000000, 'inverse': 2400000000, 'strips': 1200000000, 'finish': 1000000000, 'order': 1000000000, 'pick': 3000000000}
CHUNK = 64
PATTERN = (0, 1, 1, 0)
STEPS = (((0,), 1), ((1,), 0), ((2,), 0), ((3,), 1), ((0,), 0), ((1,), 1), ((2,), 1), ((3,), 0), ((0, 1), 2), ((2, 3), 2))


def real_tables(size):
    half = size // 2
    counter = np.arange(half)
    phase = np.outer(counter, counter) % half
    even = np.exp(-2j * np.pi * phase / half) / math.sqrt(size)
    odd = even * np.exp(-2j * np.pi * counter / size)[:, None]
    right, left = [], []
    for matrix in (even, odd):
        real = np.block([[matrix.real, matrix.imag], [-matrix.imag, matrix.real]])
        for form in (real, real.T):
            high = form.astype(ml_dtypes.bfloat16)
            low = (form - high.astype(np.float64)).astype(ml_dtypes.bfloat16)
            right.append(np.concatenate([high, high, low], 0))
            left.append(np.concatenate([high, high, low], 1))
    return np.stack(right), np.stack(left)


def split(value):
    high = value.astype(BF16)
    return high, (value - high.astype(F32)).astype(BF16)


def product(left, right):
    return jnp.dot(left, right, preferred_element_type=F32)


def put_left(ref, parity, begin, value):
    size = value.shape[1]
    lines = slice(begin, begin + value.shape[0])
    high, low = split(value)
    ref[parity, lines, :size] = high
    ref[parity, lines, size : 2 * size] = low
    ref[parity, lines, 2 * size :] = high


def put_right(ref, parity, begin, value):
    size = value.shape[1]
    high, low = split(value)
    for index, piece in enumerate((high, low, high)):
        ref[parity, index * size + begin : index * size + begin + value.shape[0]] = piece


def spans(size, count):
    return [(begin, slice(begin, begin + count)) for begin in range(0, size, count)]


def pieces_of(value):
    high, middle = split(value)
    low = (value - high.astype(F32) - middle.astype(F32)).astype(BF16)
    return high, middle, low


def prepare_kernel(probe_ref, grid_ref, own_ref):
    parts, modes, size, columns = grid_ref.shape
    lines = columns // 128
    for part in range(parts):
        for mode in range(modes):
            for line in range(lines):
                grid_ref[part, mode, :, line * 128 : (line + 1) * 128] = probe_ref[
                    part, pl.ds(line * modes + mode, size, stride=lines * modes), :
                ]
    share = own_ref.shape[1]
    own_ref[...] = probe_ref[:, pl.ds(pl.multiple_of(lax.axis_index("pos") * share, share), share), :]


def order_kernel(measured_ref, order_ref, out_ref):
    half = order_ref.shape[1] // 2
    columns, rows = order_ref[0], order_ref[1]
    for slot in range(measured_ref.shape[0]):
        value = jnp.sqrt(measured_ref[slot] + damping_factor)
        value = sum(product(piece, columns) for piece in pieces_of(value))
        value = sum(product(rows, piece) for piece in pieces_of(value))
        out_ref[slot, 0] = value[:half]
        out_ref[slot, 1] = value[half:]


def load_rows(ref, index, begin, count):
    offset = lax.rem(begin, 8)
    span = count + 8
    value = ref[(*index, pl.ds(pl.multiple_of(begin - offset, 8), span))]
    return pltpu.roll(value, lax.rem(span - offset, span), 0)[:count]


def forward_kernel(
    slot, offset_ref, own_ref, pair_ref, next_ref, pair_other_ref, next_other_ref,
    probe_ref, row_ref, col_ref, far_ref, power_ref, patch_ref, extended, left_ref, right_ref,
    middle_ref,
):
    rows = own_ref.shape[1]
    size = patch_ref.shape[1]
    position, tile = lax.axis_index("pos"), lax.axis_index("tile")
    parity = lax.rem(position, 2)
    start = offset_ref[slot, 0] - (position - 1) * rows
    extended[:, rows : 2 * rows] = own_ref[...]
    for side, mine, other in (
        (1 - parity, pair_ref, pair_other_ref),
        (parity, next_ref, next_other_ref),
    ):
        lines = pl.ds(pl.multiple_of(side * (2 * rows), rows), rows)
        extended[tile, lines] = mine[...]
        extended[1 - tile, lines] = other[...]
    for part in (0, 1):
        patch_ref[part] = load_rows(extended, (part,), start, size)
    half = size // 2
    modes = probe_ref.shape[1]

    def spread_rows(mode):
        for begin, lines in spans(size, CHUNK):
            patch_real, patch_imag = patch_ref[0, lines], patch_ref[1, lines]
            probe_real, probe_imag = probe_ref[0, mode, lines], probe_ref[1, mode, lines]
            real = probe_real * patch_real - probe_imag * patch_imag
            imag = probe_real * patch_imag + probe_imag * patch_real
            a, b = real[:, :half], real[:, half:]
            c, d = imag[:, :half], imag[:, half:]
            put_left(left_ref, 2 * (mode % 2), begin, jnp.concatenate([a + b, c + d], 1))
            put_left(left_ref, 2 * (mode % 2) + 1, begin, jnp.concatenate([a - b, c - d], 1))

    def row_products(mode):
        for parity in (0, 1):
            which = 2 * (mode % 2) + parity
            middle_ref[which] = product(left_ref[which], row_ref[2 * parity])

    def spread_columns(mode):
        first = 2 * (mode % 2)
        for begin, lines in spans(half, CHUNK // 2):
            under = slice(half + begin, half + begin + CHUNK // 2)
            for part in (0, 1):
                where = slice(part * half, (part + 1) * half)
                top = jnp.concatenate(
                    [middle_ref[first, lines, where], middle_ref[first + 1, lines, where]], 1
                )
                low = jnp.concatenate(
                    [middle_ref[first, under, where], middle_ref[first + 1, under, where]], 1
                )
                put_right(right_ref, first, part * half + begin, top + low)
                put_right(right_ref, first + 1, part * half + begin, top - low)

    def column_products(mode):
        for parity in (0, 1):
            which = 2 * (mode % 2) + parity
            far_ref[mode, parity] = product(col_ref[2 * parity + 1], right_ref[which])

    def add_power(mode):
        for parity in (0, 1):
            for begin, lines in spans(half, CHUNK):
                under = slice(half + begin, half + begin + CHUNK)
                real, imag = far_ref[mode, parity, lines], far_ref[mode, parity, under]
                power = real * real + imag * imag
                if mode == 0:
                    power_ref[parity, lines] = power
                else:
                    power_ref[parity, lines] += power

    spread_rows(0)
    row_products(0)
    for mode in range(modes):
        if mode + 1 < modes:
            spread_rows(mode + 1)
        spread_columns(mode)
        if mode + 1 < modes:
            row_products(mode + 1)
        column_products(mode)
        if mode > 0:
            add_power(mode - 1)
    add_power(modes - 1)


def block_index(block, position, bits):
    index = 0
    for bit in bits:
        differs = lax.rem(lax.div(position, 2**bit) + (block >> bit) % 2, 2)
        index = 2 * index + differs
    return index


def inverse_kernel(mode, bits, slots, fresh, start, *refs):
    count = len(slots)

    def take(number):
        nonlocal refs
        taken, refs = refs[:number], refs[number:]
        return taken

    if fresh:
        (count_ref,) = take(1)
    row_ref, col_ref, probe_ref = take(3)
    far_refs, patch_refs = take(count), take(count)
    if fresh:
        amplitude_ref, *power_refs = take(1 + 2 * count)
    else:
        ratio_refs = take(count)
        take(count)
    if not start:
        take(1)
    grad_refs, (block_ref,) = take(count), take(1)
    if fresh:
        ratio_refs = take(count)
        for index, slot in enumerate(slots):
            model = jnp.sqrt(
                power_refs[index][...] + power_refs[count + index][...] + damping_factor
            )
            active = (slot < count_ref[0]).astype(F32)
            ratio_refs[index][...] = (amplitude_ref[slot] / model - 1.0) * active
    left_ref, right_ref, middle_ref = refs
    size = probe_ref.shape[2]
    rows = block_ref.shape[3]
    half = size // 2
    position = lax.axis_index("pos")

    def spread_columns(slot, parity):
        for begin, lines in spans(half, CHUNK):
            under = slice(half + begin, half + begin + CHUNK)
            ratio = ratio_refs[slot][parity, lines]
            far = far_refs[slot].at[mode, parity]
            put_right(right_ref, 2 * slot + parity, begin, far[lines] * ratio)
            put_right(right_ref, 2 * slot + parity, half + begin, far[under] * ratio)

    def column_products(slot, parity):
        which = 2 * slot + parity
        middle_ref[which] = product(col_ref[2 * parity], right_ref[which])

    def spread_rows(slot):
        for begin, lines in spans(half, CHUNK // 2):
            under = slice(half + begin, half + begin + CHUNK // 2)
            for offset, sign in ((0, 1.0), (half, -1.0)):
                real = middle_ref[2 * slot, lines] + sign * middle_ref[2 * slot + 1, lines]
                imag = middle_ref[2 * slot, under] + sign * middle_ref[2 * slot + 1, under]
                for parity in (0, 1):
                    where = slice(parity * half, (parity + 1) * half)
                    value = jnp.concatenate([real[:, where], imag[:, where]], 1)
                    put_left(left_ref, 2 * slot + parity, offset + begin, value)

    def row_products(slot, parity):
        which = 2 * slot + parity
        middle_ref[which] = product(left_ref[which], row_ref[2 * parity + 1])

    def add_terms(slot):
        for begin, lines in spans(size, rows):
            target = block_index(begin // rows, position, bits)
            a, b = middle_ref[2 * slot, lines], middle_ref[2 * slot + 1, lines]
            plus, minus = a + b, a - b
            real = jnp.concatenate([plus[:, :half], minus[:, :half]], 1)
            imag = jnp.concatenate([plus[:, half:], minus[:, half:]], 1)
            probe_real, probe_imag = probe_ref[0, mode, lines], probe_ref[1, mode, lines]
            patch_real, patch_imag = patch_refs[slot][0, lines], patch_refs[slot][1, lines]
            grads = (
                probe_real * real + probe_imag * imag,
                probe_real * imag - probe_imag * real,
            )
            terms = (
                patch_real * real + patch_imag * imag,
                patch_real * imag - patch_imag * real,
            )
            for part in (0, 1):
                if fresh:
                    grad_refs[slot][part, lines] = grads[part]
                else:
                    grad_refs[slot][part, lines] += grads[part]
                if start and slot == 0:
                    block_ref[target, 0, part] = terms[part]
                else:
                    block_ref[target, 0, part] += terms[part]

    for slot in range(count):
        for parity in (0, 1):
            spread_columns(slot, parity)
            column_products(slot, parity)
    for slot in range(count):
        spread_rows(slot)
        if slot > 0:
            add_terms(slot - 1)
        for parity in (0, 1):
            row_products(slot, parity)
    add_terms(count - 1)


def strip_kernel(offset_ref, *refs):
    *grad_refs, keep_ref, send_ref, spread = refs
    slots, size = len(grad_refs), grad_refs[0].shape[1]
    rows = size // 2
    position, tile = lax.axis_index("pos"), lax.axis_index("tile")
    parity = lax.rem(position, 2)
    half = rows // 2
    spread[:, :, :rows] = jnp.zeros(spread.shape[:2] + (rows, size), F32)
    spread[:, :, rows + size :] = jnp.zeros(spread.shape[:2] + (rows + 8, size), F32)
    for slot in range(slots):
        spread[slot, :, rows : rows + size] = grad_refs[slot][...]
    for place, strip in enumerate((2 * (1 - parity), 2 * parity, 1)):
        for part in (0, 1):
            for ref, which in ((keep_ref, tile), (send_ref, 1 - tile)):
                total = None
                for slot in range(slots):
                    start = offset_ref[slot, 0] - (position - 1) * rows
                    begin = rows - start + strip * rows + which * half
                    value = load_rows(spread, (slot, part), begin, half)
                    total = value if total is None else total + value
                ref[place, part] = total


def finish_kernel(counts, probe_ref, strip_ref, mid_ref, pair_ref, next_ref, *refs):
    object_ref, out_ref = refs[-2:]
    half = object_ref.shape[1]
    begin = pl.multiple_of(lax.axis_index("tile") * half, half)
    object_ref[...] = strip_ref[:, pl.ds(begin, half), :] + object_step * (
        mid_ref[...] + pair_ref[...] + next_ref[...]
    )
    modes = sum(group for group, _ in counts)
    mode = 0
    for group, terms in counts:
        group_refs, refs = refs[:terms], refs[terms:]
        for index in range(group):
            for part in range(out_ref.shape[0]):
                value = sum(ref[index, part] for ref in group_refs)
                rows, columns = value.shape
                lines = columns // 128
                for line in range(lines):
                    where = pl.ds(line * modes + mode, rows, stride=lines * modes)
                    out_ref[part, where, :] = probe_ref[part, where, :] + probe_step * (
                        value[:, line * 128 : (line + 1) * 128]
                    )
            mode += 1


def pick_kernel(part_ref, out_ref):
    out_ref[...] = part_ref[...]


def call(kernel, out_shape, scalars, arrays, name, **options):
    smem = pl.BlockSpec(memory_space=pltpu.SMEM)
    vmem = pl.BlockSpec(memory_space=pltpu.VMEM)
    return pl.pallas_call(
        kernel,
        out_shape=out_shape,
        in_specs=[smem] * len(scalars) + [vmem] * len(arrays),
        out_specs=(vmem,) * len(out_shape),
        compiler_params=pltpu.CompilerParams(vmem_limit_bytes=VMEM_LIMIT),
        cost_estimate=pl.CostEstimate(flops=COSTS[name], bytes_accessed=0, transcendentals=0),
        name=name,
        **options,
    )(*scalars, *arrays)


def shape(*sizes):
    return jax.ShapeDtypeStruct(sizes, F32)


def on_device(object_field, probe, measured, offsets, counts):
    parts, strip_rows, columns = object_field.shape
    slots, size, _ = measured.shape
    modes = probe.shape[1]
    half = size // 2
    positions = lax.axis_size("pos")
    tiles = lax.axis_size("tile")
    position = lax.axis_index("pos")
    tile = lax.axis_index("tile")
    swap = [(0, 1), (1, 0)]
    pair = [(i, i ^ 1) for i in range(positions)]
    following = [(i, i + 1) for i in range(1, positions - 1, 2)]
    following += [(target, source) for source, target in following]
    tables = [jnp.asarray(table) for table in real_tables(size)]
    scratch = [
        pltpu.VMEM((4, size, 3 * size), BF16),
        pltpu.VMEM((4, 3 * size, size), BF16),
        pltpu.VMEM((4, size, size), F32),
    ]

    component = lax.dynamic_index_in_dim(object_field, tile, 0, keepdims=False)
    from_pair = lax.ppermute(component, "pos", pair)

    pixel_lines = size * size // 128
    share = pixel_lines // positions * modes
    order = np.zeros((size, size), ml_dtypes.bfloat16)
    for parity in (0, 1):
        for index in range(half):
            order[2 * index + parity, parity * half + index] = 1
    probe_lines = probe.reshape(parts, modes, pixel_lines, 128).transpose(0, 2, 1, 3)
    probe_grid, probe_own = call(
        prepare_kernel,
        (shape(parts, modes, size, size), shape(parts, share, 128)),
        [],
        [probe_lines.reshape(parts, pixel_lines * modes, 128)],
        "prepare",
    )
    (amplitude,) = call(
        order_kernel,
        (shape(slots, 2, half, size),),
        [],
        [measured, jnp.asarray(np.stack([order, order.T]))],
        "order",
    )
    (again,) = call(pick_kernel, (shape(strip_rows, columns),), [], [component], "pick")
    from_next = lax.ppermute(again, "pos", following)
    from_pair, probe_grid = lax.optimization_barrier((from_pair, probe_grid))
    pair_other = lax.ppermute(from_pair, "tile", swap)
    from_next, pair_other, amplitude = lax.optimization_barrier(
        (from_next, pair_other, amplitude)
    )
    halo = [from_pair, from_next, pair_other, lax.ppermute(from_next, "tile", swap)]

    far, power, patch = [], [], []
    for slot in range(slots):
        outs = call(
            functools.partial(forward_kernel, slot),
            (shape(modes, 2, size, size), shape(2, half, size), shape(parts, size, size)),
            [],
            [offsets, object_field, *halo, probe_grid, *tables],
            "forward",
            scratch_shapes=[pltpu.VMEM((parts, 3 * strip_rows + 8, columns), F32)] + scratch,
        )
        far.append(outs[0])
        power.append(outs[1])
        patch.append(outs[2])
    others = [lax.ppermute(value, "tile", swap) for value in power]

    block_rows = size // positions
    bit_count = positions.bit_length() - 1
    later = list(range(2, bit_count))
    every = tuple(range(slots))
    grad_shape = shape(2, size, size)
    term_shape = shape(positions, 1, 2, block_rows, size)
    grads, ratios, blocks = [], [], []
    for mode in range(modes):
        bits = [*[(1, 0), (0, 1)][PATTERN[mode % 4]], *later]
        if mode == 0:
            for slot in every:
                arrays = [*tables, probe_grid, far[slot], patch[slot]]
                arrays += [amplitude, power[slot], others[slot]]
                if slot > 0:
                    arrays.append(terms)
                grad, terms, ratio = call(
                    functools.partial(inverse_kernel, mode, bits, (slot,), True, slot == 0),
                    (grad_shape, term_shape, shape(2, half, size)),
                    [counts],
                    arrays,
                    "inverse",
                    input_output_aliases={} if slot == 0 else {len(arrays): 1},
                    scratch_shapes=scratch,
                )
                grads.append(grad)
                ratios.append(ratio)
        else:
            arrays = [*tables, probe_grid, *far, *patch, *ratios, *grads]
            *grads, terms = call(
                functools.partial(inverse_kernel, mode, bits, every, False, True),
                (grad_shape,) * slots + (term_shape,),
                [],
                arrays,
                "inverse",
                input_output_aliases={len(arrays) - slots + slot: slot for slot in every},
                scratch_shapes=scratch,
            )
        blocks.append(jnp.split(terms, 2))

    half_rows = strip_rows // tiles
    strip_shape = shape(3, parts, half_rows, columns)
    kept, sent = call(
        strip_kernel,
        (strip_shape, strip_shape),
        [],
        [offsets, *grads],
        "strips",
        scratch_shapes=[pltpu.VMEM((slots, parts, 2 * strip_rows + size + 8, columns), F32)],
    )
    strips = kept + lax.ppermute(sent, "tile", swap)
    def exchange(bit, *sends):
        payload = sends[0] if len(sends) == 1 else jnp.concatenate(sends, 0)
        got = lax.ppermute(payload, "pos", [(i, i ^ 2**bit) for i in range(positions)])
        ends = np.cumsum([send.shape[0] for send in sends])
        return [got[end - send.shape[0] : end] for send, end in zip(sends, ends)]

    def advance(modes_at, bit):
        gots = exchange(bit, *(blocks[mode][1] for mode in modes_at))
        for mode, got in zip(modes_at, gots):
            keep = blocks[mode][0]
            blocks[mode] = jnp.split(keep + got, 2) if keep.shape[0] > 1 else [keep, got]

    for modes_at, bit in STEPS:
        for now in [bit] if bit < 2 else later:
            advance(modes_at, now)
    from_pair = lax.ppermute(strips[0], "pos", pair)
    from_next = lax.ppermute(strips[1], "pos", following)
    sums = [[keep[0], got[0]] for keep, got in blocks]

    object_out, probe_out = call(
        functools.partial(finish_kernel, [(1, 2)] * modes),
        (shape(parts, half_rows, columns), shape(parts, share, 128)),
        [],
        [probe_own, object_field, strips[2], from_pair, from_next, *sum(sums, [])],
        "finish",
    )
    probe_out = probe_out.reshape(parts, share // modes, modes, 128).transpose(0, 2, 1, 3)
    return (object_out, probe_out.reshape(parts, modes, share // modes * 128))


def solution(mesh):
    in_specs = (
        P(None, ("group", "pos"), None),
        P(None, "tile", None),
        P(("group", "pos"), None, None),
        P(("group", "pos"), None),
        P(("group", "pos")),
    )
    out_specs = (P(None, ("group", "pos", "tile"), None), P(None, ("group", "tile"), "pos"))
    return jax.shard_map(
        on_device, mesh=mesh, in_specs=in_specs, out_specs=out_specs, check_vma=False
    )
```

```python
import functools
import math

import jax
import jax.numpy as jnp
import ml_dtypes
import numpy as np
from jax import lax
from jax.experimental import pallas as pl
from jax.experimental.pallas import tpu as pltpu
from jax.sharding import PartitionSpec as P

damping_factor = 0.1
object_step = 0.5
probe_step = 0.05

F32 = jnp.float32
BF16 = jnp.bfloat16
VMEM_LIMIT = 16 * 1024 * 1024
COSTS = {'prepare': 2000000000, 'forward': 4000000000, 'inverse': 2400000000, 'strips': 1200000000, 'finish': 1000000000, 'order': 1000000000, 'pick': 3000000000}
CHUNK = 64
PATTERN = (0, 1, 1, 2)
STEPS = (((0,), 1), ((1,), 0), ((2,), 0), ((3,), 1), ((0,), 2), ((1,), 1), ((3,), 0), ((2,), 1), ((0,), 0), ((1,), 2), ((2, 3), 2))


def real_tables(size):
    half = size // 2
    counter = np.arange(half)
    phase = np.outer(counter, counter) % half
    even = np.exp(-2j * np.pi * phase / half) / math.sqrt(size)
    odd = even * np.exp(-2j * np.pi * counter / size)[:, None]
    right, left = [], []
    for matrix in (even, odd):
        real = np.block([[matrix.real, matrix.imag], [-matrix.imag, matrix.real]])
        for form in (real, real.T):
            high = form.astype(ml_dtypes.bfloat16)
            low = (form - high.astype(np.float64)).astype(ml_dtypes.bfloat16)
            right.append(np.concatenate([high, high, low], 0))
            left.append(np.concatenate([high, high, low], 1))
    return np.stack(right), np.stack(left)


def split(value):
    high = value.astype(BF16)
    return high, (value - high.astype(F32)).astype(BF16)


def product(left, right):
    return jnp.dot(left, right, preferred_element_type=F32)


def put_left(ref, parity, begin, value):
    size = value.shape[1]
    lines = slice(begin, begin + value.shape[0])
    high, low = split(value)
    ref[parity, lines, :size] = high
    ref[parity, lines, size : 2 * size] = low
    ref[parity, lines, 2 * size :] = high


def put_right(ref, parity, begin, value):
    size = value.shape[1]
    high, low = split(value)
    for index, piece in enumerate((high, low, high)):
        ref[parity, index * size + begin : index * size + begin + value.shape[0]] = piece


def spans(size, count):
    return [(begin, slice(begin, begin + count)) for begin in range(0, size, count)]


def pieces_of(value):
    high, middle = split(value)
    low = (value - high.astype(F32) - middle.astype(F32)).astype(BF16)
    return high, middle, low


def prepare_kernel(probe_ref, grid_ref, own_ref):
    parts, modes, size, columns = grid_ref.shape
    lines = columns // 128
    for part in range(parts):
        for mode in range(modes):
            for line in range(lines):
                grid_ref[part, mode, :, line * 128 : (line + 1) * 128] = probe_ref[
                    part, pl.ds(line * modes + mode, size, stride=lines * modes), :
                ]
    share = own_ref.shape[1]
    own_ref[...] = probe_ref[:, pl.ds(pl.multiple_of(lax.axis_index("pos") * share, share), share), :]


def order_kernel(measured_ref, order_ref, out_ref):
    half = order_ref.shape[1] // 2
    columns, rows = order_ref[0], order_ref[1]
    for slot in range(measured_ref.shape[0]):
        value = jnp.sqrt(measured_ref[slot] + damping_factor)
        value = sum(product(piece, columns) for piece in pieces_of(value))
        value = sum(product(rows, piece) for piece in pieces_of(value))
        out_ref[slot, 0] = value[:half]
        out_ref[slot, 1] = value[half:]


def load_rows(ref, index, begin, count):
    offset = lax.rem(begin, 8)
    span = count + 8
    value = ref[(*index, pl.ds(pl.multiple_of(begin - offset, 8), span))]
    return pltpu.roll(value, lax.rem(span - offset, span), 0)[:count]


def forward_kernel(
    slot, offset_ref, own_ref, pair_ref, next_ref, pair_other_ref, next_other_ref,
    probe_ref, row_ref, col_ref, far_ref, power_ref, patch_ref, extended, left_ref, right_ref,
    middle_ref,
):
    rows = own_ref.shape[1]
    size = patch_ref.shape[1]
    position, tile = lax.axis_index("pos"), lax.axis_index("tile")
    parity = lax.rem(position, 2)
    start = offset_ref[slot, 0] - (position - 1) * rows
    extended[:, rows : 2 * rows] = own_ref[...]
    for side, mine, other in (
        (1 - parity, pair_ref, pair_other_ref),
        (parity, next_ref, next_other_ref),
    ):
        lines = pl.ds(pl.multiple_of(side * (2 * rows), rows), rows)
        extended[tile, lines] = mine[...]
        extended[1 - tile, lines] = other[...]
    for part in (0, 1):
        patch_ref[part] = load_rows(extended, (part,), start, size)
    half = size // 2
    modes = probe_ref.shape[1]

    def spread_rows(mode):
        for begin, lines in spans(size, CHUNK):
            patch_real, patch_imag = patch_ref[0, lines], patch_ref[1, lines]
            probe_real, probe_imag = probe_ref[0, mode, lines], probe_ref[1, mode, lines]
            real = probe_real * patch_real - probe_imag * patch_imag
            imag = probe_real * patch_imag + probe_imag * patch_real
            a, b = real[:, :half], real[:, half:]
            c, d = imag[:, :half], imag[:, half:]
            put_left(left_ref, 2 * (mode % 2), begin, jnp.concatenate([a + b, c + d], 1))
            put_left(left_ref, 2 * (mode % 2) + 1, begin, jnp.concatenate([a - b, c - d], 1))

    def row_products(mode):
        for parity in (0, 1):
            which = 2 * (mode % 2) + parity
            middle_ref[which] = product(left_ref[which], row_ref[2 * parity])

    def spread_columns(mode):
        first = 2 * (mode % 2)
        for begin, lines in spans(half, CHUNK // 2):
            under = slice(half + begin, half + begin + CHUNK // 2)
            for part in (0, 1):
                where = slice(part * half, (part + 1) * half)
                top = jnp.concatenate(
                    [middle_ref[first, lines, where], middle_ref[first + 1, lines, where]], 1
                )
                low = jnp.concatenate(
                    [middle_ref[first, under, where], middle_ref[first + 1, under, where]], 1
                )
                put_right(right_ref, first, part * half + begin, top + low)
                put_right(right_ref, first + 1, part * half + begin, top - low)

    def column_products(mode):
        for parity in (0, 1):
            which = 2 * (mode % 2) + parity
            far_ref[mode, parity] = product(col_ref[2 * parity + 1], right_ref[which])

    def add_power(mode):
        for parity in (0, 1):
            for begin, lines in spans(half, CHUNK):
                under = slice(half + begin, half + begin + CHUNK)
                real, imag = far_ref[mode, parity, lines], far_ref[mode, parity, under]
                power = real * real + imag * imag
                if mode == 0:
                    power_ref[parity, lines] = power
                else:
                    power_ref[parity, lines] += power

    spread_rows(0)
    row_products(0)
    for mode in range(modes):
        if mode + 1 < modes:
            spread_rows(mode + 1)
        spread_columns(mode)
        if mode + 1 < modes:
            row_products(mode + 1)
        column_products(mode)
        if mode > 0:
            add_power(mode - 1)
    add_power(modes - 1)


def block_index(block, position, bits):
    index = 0
    for bit in bits:
        differs = lax.rem(lax.div(position, 2**bit) + (block >> bit) % 2, 2)
        index = 2 * index + differs
    return index


def inverse_kernel(mode, bits, slots, fresh, start, *refs):
    count = len(slots)

    def take(number):
        nonlocal refs
        taken, refs = refs[:number], refs[number:]
        return taken

    if fresh:
        (count_ref,) = take(1)
    row_ref, col_ref, probe_ref = take(3)
    far_refs, patch_refs = take(count), take(count)
    if fresh:
        amplitude_ref, *power_refs = take(1 + 2 * count)
    else:
        ratio_refs = take(count)
        take(count)
    if not start:
        take(1)
    grad_refs, (block_ref,) = take(count), take(1)
    if fresh:
        ratio_refs = take(count)
        for index, slot in enumerate(slots):
            model = jnp.sqrt(
                power_refs[index][...] + power_refs[count + index][...] + damping_factor
            )
            active = (slot < count_ref[0]).astype(F32)
            ratio_refs[index][...] = (amplitude_ref[slot] / model - 1.0) * active
    left_ref, right_ref, middle_ref = refs
    size = probe_ref.shape[2]
    rows = block_ref.shape[3]
    half = size // 2
    position = lax.axis_index("pos")

    def spread_columns(slot, parity):
        for begin, lines in spans(half, CHUNK):
            under = slice(half + begin, half + begin + CHUNK)
            ratio = ratio_refs[slot][parity, lines]
            far = far_refs[slot].at[mode, parity]
            put_right(right_ref, 2 * slot + parity, begin, far[lines] * ratio)
            put_right(right_ref, 2 * slot + parity, half + begin, far[under] * ratio)

    def column_products(slot, parity):
        which = 2 * slot + parity
        middle_ref[which] = product(col_ref[2 * parity], right_ref[which])

    def spread_rows(slot):
        for begin, lines in spans(half, CHUNK // 2):
            under = slice(half + begin, half + begin + CHUNK // 2)
            for offset, sign in ((0, 1.0), (half, -1.0)):
                real = middle_ref[2 * slot, lines] + sign * middle_ref[2 * slot + 1, lines]
                imag = middle_ref[2 * slot, under] + sign * middle_ref[2 * slot + 1, under]
                for parity in (0, 1):
                    where = slice(parity * half, (parity + 1) * half)
                    value = jnp.concatenate([real[:, where], imag[:, where]], 1)
                    put_left(left_ref, 2 * slot + parity, offset + begin, value)

    def row_products(slot, parity):
        which = 2 * slot + parity
        middle_ref[which] = product(left_ref[which], row_ref[2 * parity + 1])

    def add_terms(slot):
        for begin, lines in spans(size, rows):
            target = block_index(begin // rows, position, bits)
            a, b = middle_ref[2 * slot, lines], middle_ref[2 * slot + 1, lines]
            plus, minus = a + b, a - b
            real = jnp.concatenate([plus[:, :half], minus[:, :half]], 1)
            imag = jnp.concatenate([plus[:, half:], minus[:, half:]], 1)
            probe_real, probe_imag = probe_ref[0, mode, lines], probe_ref[1, mode, lines]
            patch_real, patch_imag = patch_refs[slot][0, lines], patch_refs[slot][1, lines]
            grads = (
                probe_real * real + probe_imag * imag,
                probe_real * imag - probe_imag * real,
            )
            terms = (
                patch_real * real + patch_imag * imag,
                patch_real * imag - patch_imag * real,
            )
            for part in (0, 1):
                if fresh:
                    grad_refs[slot][part, lines] = grads[part]
                else:
                    grad_refs[slot][part, lines] += grads[part]
                if start and slot == 0:
                    block_ref[target, 0, part] = terms[part]
                else:
                    block_ref[target, 0, part] += terms[part]

    for slot in range(count):
        for parity in (0, 1):
            spread_columns(slot, parity)
            column_products(slot, parity)
    for slot in range(count):
        spread_rows(slot)
        if slot > 0:
            add_terms(slot - 1)
        for parity in (0, 1):
            row_products(slot, parity)
    add_terms(count - 1)


def strip_kernel(offset_ref, *refs):
    *grad_refs, keep_ref, send_ref, spread = refs
    slots, size = len(grad_refs), grad_refs[0].shape[1]
    rows = size // 2
    position, tile = lax.axis_index("pos"), lax.axis_index("tile")
    parity = lax.rem(position, 2)
    half = rows // 2
    spread[:, :, :rows] = jnp.zeros(spread.shape[:2] + (rows, size), F32)
    spread[:, :, rows + size :] = jnp.zeros(spread.shape[:2] + (rows + 8, size), F32)
    for slot in range(slots):
        spread[slot, :, rows : rows + size] = grad_refs[slot][...]
    for place, strip in enumerate((2 * (1 - parity), 2 * parity, 1)):
        for part in (0, 1):
            for ref, which in ((keep_ref, tile), (send_ref, 1 - tile)):
                total = None
                for slot in range(slots):
                    start = offset_ref[slot, 0] - (position - 1) * rows
                    begin = rows - start + strip * rows + which * half
                    value = load_rows(spread, (slot, part), begin, half)
                    total = value if total is None else total + value
                ref[place, part] = total


def finish_kernel(counts, probe_ref, strip_ref, mid_ref, pair_ref, next_ref, *refs):
    object_ref, out_ref = refs[-2:]
    half = object_ref.shape[1]
    begin = pl.multiple_of(lax.axis_index("tile") * half, half)
    object_ref[...] = strip_ref[:, pl.ds(begin, half), :] + object_step * (
        mid_ref[...] + pair_ref[...] + next_ref[...]
    )
    modes = sum(group for group, _ in counts)
    mode = 0
    for group, terms in counts:
        group_refs, refs = refs[:terms], refs[terms:]
        for index in range(group):
            for part in range(out_ref.shape[0]):
                value = sum(ref[index, part] for ref in group_refs)
                rows, columns = value.shape
                lines = columns // 128
                for line in range(lines):
                    where = pl.ds(line * modes + mode, rows, stride=lines * modes)
                    out_ref[part, where, :] = probe_ref[part, where, :] + probe_step * (
                        value[:, line * 128 : (line + 1) * 128]
                    )
            mode += 1


def pick_kernel(part_ref, out_ref):
    out_ref[...] = part_ref[...]


def call(kernel, out_shape, scalars, arrays, name, **options):
    smem = pl.BlockSpec(memory_space=pltpu.SMEM)
    vmem = pl.BlockSpec(memory_space=pltpu.VMEM)
    return pl.pallas_call(
        kernel,
        out_shape=out_shape,
        in_specs=[smem] * len(scalars) + [vmem] * len(arrays),
        out_specs=(vmem,) * len(out_shape),
        compiler_params=pltpu.CompilerParams(vmem_limit_bytes=VMEM_LIMIT),
        cost_estimate=pl.CostEstimate(flops=COSTS[name], bytes_accessed=0, transcendentals=0),
        name=name,
        **options,
    )(*scalars, *arrays)


def shape(*sizes):
    return jax.ShapeDtypeStruct(sizes, F32)


def on_device(object_field, probe, measured, offsets, counts):
    parts, strip_rows, columns = object_field.shape
    slots, size, _ = measured.shape
    modes = probe.shape[1]
    half = size // 2
    positions = lax.axis_size("pos")
    tiles = lax.axis_size("tile")
    position = lax.axis_index("pos")
    tile = lax.axis_index("tile")
    swap = [(0, 1), (1, 0)]
    pair = [(i, i ^ 1) for i in range(positions)]
    following = [(i, i + 1) for i in range(1, positions - 1, 2)]
    following += [(target, source) for source, target in following]
    tables = [jnp.asarray(table) for table in real_tables(size)]
    scratch = [
        pltpu.VMEM((4, size, 3 * size), BF16),
        pltpu.VMEM((4, 3 * size, size), BF16),
        pltpu.VMEM((4, size, size), F32),
    ]

    component = lax.dynamic_index_in_dim(object_field, tile, 0, keepdims=False)
    from_pair = lax.ppermute(component, "pos", pair)

    pixel_lines = size * size // 128
    share = pixel_lines // positions * modes
    order = np.zeros((size, size), ml_dtypes.bfloat16)
    for parity in (0, 1):
        for index in range(half):
            order[2 * index + parity, parity * half + index] = 1
    probe_lines = probe.reshape(parts, modes, pixel_lines, 128).transpose(0, 2, 1, 3)
    probe_grid, probe_own = call(
        prepare_kernel,
        (shape(parts, modes, size, size), shape(parts, share, 128)),
        [],
        [probe_lines.reshape(parts, pixel_lines * modes, 128)],
        "prepare",
    )
    (amplitude,) = call(
        order_kernel,
        (shape(slots, 2, half, size),),
        [],
        [measured, jnp.asarray(np.stack([order, order.T]))],
        "order",
    )
    (again,) = call(pick_kernel, (shape(strip_rows, columns),), [], [component], "pick")
    from_next = lax.ppermute(again, "pos", following)
    from_pair, probe_grid = lax.optimization_barrier((from_pair, probe_grid))
    pair_other = lax.ppermute(from_pair, "tile", swap)
    from_next, pair_other, amplitude = lax.optimization_barrier(
        (from_next, pair_other, amplitude)
    )
    halo = [from_pair, from_next, pair_other, lax.ppermute(from_next, "tile", swap)]

    far, power, patch = [], [], []
    for slot in range(slots):
        outs = call(
            functools.partial(forward_kernel, slot),
            (shape(modes, 2, size, size), shape(2, half, size), shape(parts, size, size)),
            [],
            [offsets, object_field, *halo, probe_grid, *tables],
            "forward",
            scratch_shapes=[pltpu.VMEM((parts, 3 * strip_rows + 8, columns), F32)] + scratch,
        )
        far.append(outs[0])
        power.append(outs[1])
        patch.append(outs[2])
    others = [lax.ppermute(value, "tile", swap) for value in power]

    block_rows = size // positions
    bit_count = positions.bit_length() - 1
    later = list(range(2, bit_count))
    every = tuple(range(slots))
    grad_shape = shape(2, size, size)
    term_shape = shape(positions, 1, 2, block_rows, size)
    grads, ratios, blocks = [], [], []
    for mode in range(modes):
        bits = [(1, *later, 0), (0, 1, *later), (1, 0, *later)][PATTERN[mode % 4]]
        if mode == 0:
            for slot in every:
                arrays = [*tables, probe_grid, far[slot], patch[slot]]
                arrays += [amplitude, power[slot], others[slot]]
                if slot > 0:
                    arrays.append(terms)
                grad, terms, ratio = call(
                    functools.partial(inverse_kernel, mode, bits, (slot,), True, slot == 0),
                    (grad_shape, term_shape, shape(2, half, size)),
                    [counts],
                    arrays,
                    "inverse",
                    input_output_aliases={} if slot == 0 else {len(arrays): 1},
                    scratch_shapes=scratch,
                )
                grads.append(grad)
                ratios.append(ratio)
        else:
            arrays = [*tables, probe_grid, *far, *patch, *ratios, *grads]
            *grads, terms = call(
                functools.partial(inverse_kernel, mode, bits, every, False, True),
                (grad_shape,) * slots + (term_shape,),
                [],
                arrays,
                "inverse",
                input_output_aliases={len(arrays) - slots + slot: slot for slot in every},
                scratch_shapes=scratch,
            )
        blocks.append(jnp.split(terms, 2))

    half_rows = strip_rows // tiles
    strip_shape = shape(3, parts, half_rows, columns)
    kept, sent = call(
        strip_kernel,
        (strip_shape, strip_shape),
        [],
        [offsets, *grads],
        "strips",
        scratch_shapes=[pltpu.VMEM((slots, parts, 2 * strip_rows + size + 8, columns), F32)],
    )
    strips = kept + lax.ppermute(sent, "tile", swap)
    def exchange(bit, *sends):
        payload = sends[0] if len(sends) == 1 else jnp.concatenate(sends, 0)
        got = lax.ppermute(payload, "pos", [(i, i ^ 2**bit) for i in range(positions)])
        ends = np.cumsum([send.shape[0] for send in sends])
        return [got[end - send.shape[0] : end] for send, end in zip(sends, ends)]

    def advance(modes_at, bit):
        gots = exchange(bit, *(blocks[mode][1] for mode in modes_at))
        for mode, got in zip(modes_at, gots):
            keep = blocks[mode][0]
            blocks[mode] = jnp.split(keep + got, 2) if keep.shape[0] > 1 else [keep, got]

    for modes_at, bit in STEPS:
        for now in [bit] if bit < 2 else later:
            advance(modes_at, now)
    from_pair = lax.ppermute(strips[0], "pos", pair)
    from_next = lax.ppermute(strips[1], "pos", following)
    sums = [[keep[0], got[0]] for keep, got in blocks]

    object_out, probe_out = call(
        functools.partial(finish_kernel, [(1, 2)] * modes),
        (shape(parts, half_rows, columns), shape(parts, share, 128)),
        [],
        [probe_own, object_field, strips[2], from_pair, from_next, *sum(sums, [])],
        "finish",
    )
    probe_out = probe_out.reshape(parts, share // modes, modes, 128).transpose(0, 2, 1, 3)
    return (object_out, probe_out.reshape(parts, modes, share // modes * 128))


def solution(mesh):
    in_specs = (
        P(None, ("group", "pos"), None),
        P(None, "tile", None),
        P(("group", "pos"), None, None),
        P(("group", "pos"), None),
        P(("group", "pos")),
    )
    out_specs = (P(None, ("group", "pos", "tile"), None), P(None, ("group", "tile"), "pos"))
    return jax.shard_map(
        on_device, mesh=mesh, in_specs=in_specs, out_specs=out_specs, check_vma=False
    )
```

```python
import functools
import math

import jax
import jax.numpy as jnp
import ml_dtypes
import numpy as np
from jax import lax
from jax.experimental import pallas as pl
from jax.experimental.pallas import tpu as pltpu
from jax.sharding import PartitionSpec as P

damping_factor = 0.1
object_step = 0.5
probe_step = 0.05

F32 = jnp.float32
BF16 = jnp.bfloat16
VMEM_LIMIT = 16 * 1024 * 1024
COSTS = {'prepare': 2000000000, 'forward': 4000000000, 'inverse': 2400000000, 'strips': 1200000000, 'finish': 1000000000, 'order': 1000000000, 'pick': 3000000000}
CHUNK = 128
PATTERN = (0, 1, 1, 2)
STEPS = (((0,), 1), ((1,), 0), ((2,), 0), ((3,), 1), ((0,), 2), ((1,), 1), ((3,), 0), ((2,), 1), ((0,), 0), ((1,), 2), ((2, 3), 2))


def real_tables(size):
    half = size // 2
    counter = np.arange(half)
    phase = np.outer(counter, counter) % half
    even = np.exp(-2j * np.pi * phase / half) / math.sqrt(size)
    odd = even * np.exp(-2j * np.pi * counter / size)[:, None]
    right, left = [], []
    for matrix in (even, odd):
        real = np.block([[matrix.real, matrix.imag], [-matrix.imag, matrix.real]])
        for form in (real, real.T):
            high = form.astype(ml_dtypes.bfloat16)
            low = (form - high.astype(np.float64)).astype(ml_dtypes.bfloat16)
            right.append(np.concatenate([high, high, low], 0))
            left.append(np.concatenate([high, high, low], 1))
    return np.stack(right), np.stack(left)


def split(value):
    high = value.astype(BF16)
    return high, (value - high.astype(F32)).astype(BF16)


def product(left, right):
    return jnp.dot(left, right, preferred_element_type=F32)


def put_left(ref, parity, begin, value):
    size = value.shape[1]
    lines = slice(begin, begin + value.shape[0])
    high, low = split(value)
    ref[parity, lines, :size] = high
    ref[parity, lines, size : 2 * size] = low
    ref[parity, lines, 2 * size :] = high


def put_right(ref, parity, begin, value):
    size = value.shape[1]
    high, low = split(value)
    for index, piece in enumerate((high, low, high)):
        ref[parity, index * size + begin : index * size + begin + value.shape[0]] = piece


def spans(size, count):
    return [(begin, slice(begin, begin + count)) for begin in range(0, size, count)]


def pieces_of(value):
    high, middle = split(value)
    low = (value - high.astype(F32) - middle.astype(F32)).astype(BF16)
    return high, middle, low


def prepare_kernel(probe_ref, grid_ref, own_ref):
    parts, modes, size, columns = grid_ref.shape
    lines = columns // 128
    for part in range(parts):
        for mode in range(modes):
            for line in range(lines):
                grid_ref[part, mode, :, line * 128 : (line + 1) * 128] = probe_ref[
                    part, pl.ds(line * modes + mode, size, stride=lines * modes), :
                ]
    share = own_ref.shape[1]
    own_ref[...] = probe_ref[:, pl.ds(pl.multiple_of(lax.axis_index("pos") * share, share), share), :]


def order_kernel(measured_ref, order_ref, out_ref):
    half = order_ref.shape[1] // 2
    columns, rows = order_ref[0], order_ref[1]
    for slot in range(measured_ref.shape[0]):
        value = jnp.sqrt(measured_ref[slot] + damping_factor)
        value = sum(product(piece, columns) for piece in pieces_of(value))
        value = sum(product(rows, piece) for piece in pieces_of(value))
        out_ref[slot, 0] = value[:half]
        out_ref[slot, 1] = value[half:]


def load_rows(ref, index, begin, count):
    offset = lax.rem(begin, 8)
    span = count + 8
    value = ref[(*index, pl.ds(pl.multiple_of(begin - offset, 8), span))]
    return pltpu.roll(value, lax.rem(span - offset, span), 0)[:count]


def forward_kernel(
    slot, offset_ref, own_ref, pair_ref, next_ref, pair_other_ref, next_other_ref,
    probe_ref, row_ref, col_ref, far_ref, power_ref, patch_ref, extended, left_ref, right_ref,
    middle_ref,
):
    rows = own_ref.shape[1]
    size = patch_ref.shape[1]
    position, tile = lax.axis_index("pos"), lax.axis_index("tile")
    parity = lax.rem(position, 2)
    start = offset_ref[slot, 0] - (position - 1) * rows
    extended[:, rows : 2 * rows] = own_ref[...]
    for side, mine, other in (
        (1 - parity, pair_ref, pair_other_ref),
        (parity, next_ref, next_other_ref),
    ):
        lines = pl.ds(pl.multiple_of(side * (2 * rows), rows), rows)
        extended[tile, lines] = mine[...]
        extended[1 - tile, lines] = other[...]
    for part in (0, 1):
        patch_ref[part] = load_rows(extended, (part,), start, size)
    half = size // 2
    modes = probe_ref.shape[1]

    def spread_rows(mode):
        for begin, lines in spans(size, CHUNK):
            patch_real, patch_imag = patch_ref[0, lines], patch_ref[1, lines]
            probe_real, probe_imag = probe_ref[0, mode, lines], probe_ref[1, mode, lines]
            real = probe_real * patch_real - probe_imag * patch_imag
            imag = probe_real * patch_imag + probe_imag * patch_real
            a, b = real[:, :half], real[:, half:]
            c, d = imag[:, :half], imag[:, half:]
            put_left(left_ref, 2 * (mode % 2), begin, jnp.concatenate([a + b, c + d], 1))
            put_left(left_ref, 2 * (mode % 2) + 1, begin, jnp.concatenate([a - b, c - d], 1))

    def row_products(mode):
        for parity in (0, 1):
            which = 2 * (mode % 2) + parity
            middle_ref[which] = product(left_ref[which], row_ref[2 * parity])

    def spread_columns(mode):
        first = 2 * (mode % 2)
        for begin, lines in spans(half, CHUNK // 2):
            under = slice(half + begin, half + begin + CHUNK // 2)
            for part in (0, 1):
                where = slice(part * half, (part + 1) * half)
                top = jnp.concatenate(
                    [middle_ref[first, lines, where], middle_ref[first + 1, lines, where]], 1
                )
                low = jnp.concatenate(
                    [middle_ref[first, under, where], middle_ref[first + 1, under, where]], 1
                )
                put_right(right_ref, first, part * half + begin, top + low)
                put_right(right_ref, first + 1, part * half + begin, top - low)

    def column_products(mode):
        for parity in (0, 1):
            which = 2 * (mode % 2) + parity
            far_ref[mode, parity] = product(col_ref[2 * parity + 1], right_ref[which])

    def add_power(mode):
        for parity in (0, 1):
            for begin, lines in spans(half, CHUNK):
                under = slice(half + begin, half + begin + CHUNK)
                real, imag = far_ref[mode, parity, lines], far_ref[mode, parity, under]
                power = real * real + imag * imag
                if mode == 0:
                    power_ref[parity, lines] = power
                else:
                    power_ref[parity, lines] += power

    spread_rows(0)
    row_products(0)
    for mode in range(modes):
        if mode + 1 < modes:
            spread_rows(mode + 1)
        spread_columns(mode)
        if mode + 1 < modes:
            row_products(mode + 1)
        column_products(mode)
        if mode > 0:
            add_power(mode - 1)
    add_power(modes - 1)


def block_index(block, position, bits):
    index = 0
    for bit in bits:
        differs = lax.rem(lax.div(position, 2**bit) + (block >> bit) % 2, 2)
        index = 2 * index + differs
    return index


def inverse_kernel(mode, bits, slots, fresh, start, *refs):
    count = len(slots)

    def take(number):
        nonlocal refs
        taken, refs = refs[:number], refs[number:]
        return taken

    if fresh:
        (count_ref,) = take(1)
    row_ref, col_ref, probe_ref = take(3)
    far_refs, patch_refs = take(count), take(count)
    if fresh:
        amplitude_ref, *power_refs = take(1 + 2 * count)
    else:
        ratio_refs = take(count)
        take(count)
    if not start:
        take(1)
    grad_refs, (block_ref,) = take(count), take(1)
    if fresh:
        ratio_refs = take(count)
        for index, slot in enumerate(slots):
            model = jnp.sqrt(
                power_refs[index][...] + power_refs[count + index][...] + damping_factor
            )
            active = (slot < count_ref[0]).astype(F32)
            ratio_refs[index][...] = (amplitude_ref[slot] / model - 1.0) * active
    left_ref, right_ref, middle_ref = refs
    size = probe_ref.shape[2]
    rows = block_ref.shape[3]
    half = size // 2
    position = lax.axis_index("pos")

    def spread_columns(slot, parity):
        for begin, lines in spans(half, CHUNK):
            under = slice(half + begin, half + begin + CHUNK)
            ratio = ratio_refs[slot][parity, lines]
            far = far_refs[slot].at[mode, parity]
            put_right(right_ref, 2 * slot + parity, begin, far[lines] * ratio)
            put_right(right_ref, 2 * slot + parity, half + begin, far[under] * ratio)

    def column_products(slot, parity):
        which = 2 * slot + parity
        middle_ref[which] = product(col_ref[2 * parity], right_ref[which])

    def spread_rows(slot):
        for begin, lines in spans(half, CHUNK // 2):
            under = slice(half + begin, half + begin + CHUNK // 2)
            for offset, sign in ((0, 1.0), (half, -1.0)):
                real = middle_ref[2 * slot, lines] + sign * middle_ref[2 * slot + 1, lines]
                imag = middle_ref[2 * slot, under] + sign * middle_ref[2 * slot + 1, under]
                for parity in (0, 1):
                    where = slice(parity * half, (parity + 1) * half)
                    value = jnp.concatenate([real[:, where], imag[:, where]], 1)
                    put_left(left_ref, 2 * slot + parity, offset + begin, value)

    def row_products(slot, parity):
        which = 2 * slot + parity
        middle_ref[which] = product(left_ref[which], row_ref[2 * parity + 1])

    def add_terms(slot):
        for begin, lines in spans(size, rows):
            target = block_index(begin // rows, position, bits)
            a, b = middle_ref[2 * slot, lines], middle_ref[2 * slot + 1, lines]
            plus, minus = a + b, a - b
            real = jnp.concatenate([plus[:, :half], minus[:, :half]], 1)
            imag = jnp.concatenate([plus[:, half:], minus[:, half:]], 1)
            probe_real, probe_imag = probe_ref[0, mode, lines], probe_ref[1, mode, lines]
            patch_real, patch_imag = patch_refs[slot][0, lines], patch_refs[slot][1, lines]
            grads = (
                probe_real * real + probe_imag * imag,
                probe_real * imag - probe_imag * real,
            )
            terms = (
                patch_real * real + patch_imag * imag,
                patch_real * imag - patch_imag * real,
            )
            for part in (0, 1):
                if fresh:
                    grad_refs[slot][part, lines] = grads[part]
                else:
                    grad_refs[slot][part, lines] += grads[part]
                if start and slot == 0:
                    block_ref[target, 0, part] = terms[part]
                else:
                    block_ref[target, 0, part] += terms[part]

    for slot in range(count):
        for parity in (0, 1):
            spread_columns(slot, parity)
            column_products(slot, parity)
    for slot in range(count):
        spread_rows(slot)
        if slot > 0:
            add_terms(slot - 1)
        for parity in (0, 1):
            row_products(slot, parity)
    add_terms(count - 1)


def strip_kernel(offset_ref, *refs):
    *grad_refs, keep_ref, send_ref, spread = refs
    slots, size = len(grad_refs), grad_refs[0].shape[1]
    rows = size // 2
    position, tile = lax.axis_index("pos"), lax.axis_index("tile")
    parity = lax.rem(position, 2)
    half = rows // 2
    spread[:, :, :rows] = jnp.zeros(spread.shape[:2] + (rows, size), F32)
    spread[:, :, rows + size :] = jnp.zeros(spread.shape[:2] + (rows + 8, size), F32)
    for slot in range(slots):
        spread[slot, :, rows : rows + size] = grad_refs[slot][...]
    for place, strip in enumerate((2 * (1 - parity), 2 * parity, 1)):
        for part in (0, 1):
            for ref, which in ((keep_ref, tile), (send_ref, 1 - tile)):
                total = None
                for slot in range(slots):
                    start = offset_ref[slot, 0] - (position - 1) * rows
                    begin = rows - start + strip * rows + which * half
                    value = load_rows(spread, (slot, part), begin, half)
                    total = value if total is None else total + value
                ref[place, part] = total


def finish_kernel(counts, probe_ref, strip_ref, mid_ref, pair_ref, next_ref, *refs):
    object_ref, out_ref = refs[-2:]
    half = object_ref.shape[1]
    begin = pl.multiple_of(lax.axis_index("tile") * half, half)
    object_ref[...] = strip_ref[:, pl.ds(begin, half), :] + object_step * (
        mid_ref[...] + pair_ref[...] + next_ref[...]
    )
    modes = sum(group for group, _ in counts)
    mode = 0
    for group, terms in counts:
        group_refs, refs = refs[:terms], refs[terms:]
        for index in range(group):
            for part in range(out_ref.shape[0]):
                value = sum(ref[index, part] for ref in group_refs)
                rows, columns = value.shape
                lines = columns // 128
                for line in range(lines):
                    where = pl.ds(line * modes + mode, rows, stride=lines * modes)
                    out_ref[part, where, :] = probe_ref[part, where, :] + probe_step * (
                        value[:, line * 128 : (line + 1) * 128]
                    )
            mode += 1


def pick_kernel(part_ref, out_ref):
    out_ref[...] = part_ref[...]


def call(kernel, out_shape, scalars, arrays, name, **options):
    smem = pl.BlockSpec(memory_space=pltpu.SMEM)
    vmem = pl.BlockSpec(memory_space=pltpu.VMEM)
    return pl.pallas_call(
        kernel,
        out_shape=out_shape,
        in_specs=[smem] * len(scalars) + [vmem] * len(arrays),
        out_specs=(vmem,) * len(out_shape),
        compiler_params=pltpu.CompilerParams(vmem_limit_bytes=VMEM_LIMIT),
        cost_estimate=pl.CostEstimate(flops=COSTS[name], bytes_accessed=0, transcendentals=0),
        name=name,
        **options,
    )(*scalars, *arrays)


def shape(*sizes):
    return jax.ShapeDtypeStruct(sizes, F32)


def on_device(object_field, probe, measured, offsets, counts):
    parts, strip_rows, columns = object_field.shape
    slots, size, _ = measured.shape
    modes = probe.shape[1]
    half = size // 2
    positions = lax.axis_size("pos")
    tiles = lax.axis_size("tile")
    position = lax.axis_index("pos")
    tile = lax.axis_index("tile")
    swap = [(0, 1), (1, 0)]
    pair = [(i, i ^ 1) for i in range(positions)]
    following = [(i, i + 1) for i in range(1, positions - 1, 2)]
    following += [(target, source) for source, target in following]
    tables = [jnp.asarray(table) for table in real_tables(size)]
    scratch = [
        pltpu.VMEM((4, size, 3 * size), BF16),
        pltpu.VMEM((4, 3 * size, size), BF16),
        pltpu.VMEM((4, size, size), F32),
    ]

    component = lax.dynamic_index_in_dim(object_field, tile, 0, keepdims=False)
    from_pair = lax.ppermute(component, "pos", pair)

    pixel_lines = size * size // 128
    share = pixel_lines // positions * modes
    order = np.zeros((size, size), ml_dtypes.bfloat16)
    for parity in (0, 1):
        for index in range(half):
            order[2 * index + parity, parity * half + index] = 1
    probe_lines = probe.reshape(parts, modes, pixel_lines, 128).transpose(0, 2, 1, 3)
    probe_grid, probe_own = call(
        prepare_kernel,
        (shape(parts, modes, size, size), shape(parts, share, 128)),
        [],
        [probe_lines.reshape(parts, pixel_lines * modes, 128)],
        "prepare",
    )
    (amplitude,) = call(
        order_kernel,
        (shape(slots, 2, half, size),),
        [],
        [measured, jnp.asarray(np.stack([order, order.T]))],
        "order",
    )
    (again,) = call(pick_kernel, (shape(strip_rows, columns),), [], [component], "pick")
    from_next = lax.ppermute(again, "pos", following)
    from_pair, probe_grid = lax.optimization_barrier((from_pair, probe_grid))
    pair_other = lax.ppermute(from_pair, "tile", swap)
    from_next, pair_other, amplitude = lax.optimization_barrier(
        (from_next, pair_other, amplitude)
    )
    halo = [from_pair, from_next, pair_other, lax.ppermute(from_next, "tile", swap)]

    far, power, patch = [], [], []
    for slot in range(slots):
        outs = call(
            functools.partial(forward_kernel, slot),
            (shape(modes, 2, size, size), shape(2, half, size), shape(parts, size, size)),
            [],
            [offsets, object_field, *halo, probe_grid, *tables],
            "forward",
            scratch_shapes=[pltpu.VMEM((parts, 3 * strip_rows + 8, columns), F32)] + scratch,
        )
        far.append(outs[0])
        power.append(outs[1])
        patch.append(outs[2])
    others = [lax.ppermute(value, "tile", swap) for value in power]

    block_rows = size // positions
    bit_count = positions.bit_length() - 1
    later = list(range(2, bit_count))
    every = tuple(range(slots))
    grad_shape = shape(2, size, size)
    term_shape = shape(positions, 1, 2, block_rows, size)
    grads, ratios, blocks = [], [], []
    for mode in range(modes):
        bits = [(1, *later, 0), (0, 1, *later), (1, 0, *later)][PATTERN[mode % 4]]
        if mode == 0:
            for slot in every:
                arrays = [*tables, probe_grid, far[slot], patch[slot]]
                arrays += [amplitude, power[slot], others[slot]]
                if slot > 0:
                    arrays.append(terms)
                grad, terms, ratio = call(
                    functools.partial(inverse_kernel, mode, bits, (slot,), True, slot == 0),
                    (grad_shape, term_shape, shape(2, half, size)),
                    [counts],
                    arrays,
                    "inverse",
                    input_output_aliases={} if slot == 0 else {len(arrays): 1},
                    scratch_shapes=scratch,
                )
                grads.append(grad)
                ratios.append(ratio)
        else:
            arrays = [*tables, probe_grid, *far, *patch, *ratios, *grads]
            *grads, terms = call(
                functools.partial(inverse_kernel, mode, bits, every, False, True),
                (grad_shape,) * slots + (term_shape,),
                [],
                arrays,
                "inverse",
                input_output_aliases={len(arrays) - slots + slot: slot for slot in every},
                scratch_shapes=scratch,
            )
        blocks.append(jnp.split(terms, 2))

    half_rows = strip_rows // tiles
    strip_shape = shape(3, parts, half_rows, columns)
    kept, sent = call(
        strip_kernel,
        (strip_shape, strip_shape),
        [],
        [offsets, *grads],
        "strips",
        scratch_shapes=[pltpu.VMEM((slots, parts, 2 * strip_rows + size + 8, columns), F32)],
    )
    strips = kept + lax.ppermute(sent, "tile", swap)
    def exchange(bit, *sends):
        payload = sends[0] if len(sends) == 1 else jnp.concatenate(sends, 0)
        got = lax.ppermute(payload, "pos", [(i, i ^ 2**bit) for i in range(positions)])
        ends = np.cumsum([send.shape[0] for send in sends])
        return [got[end - send.shape[0] : end] for send, end in zip(sends, ends)]

    def advance(modes_at, bit):
        gots = exchange(bit, *(blocks[mode][1] for mode in modes_at))
        for mode, got in zip(modes_at, gots):
            keep = blocks[mode][0]
            blocks[mode] = jnp.split(keep + got, 2) if keep.shape[0] > 1 else [keep, got]

    for modes_at, bit in STEPS:
        for now in [bit] if bit < 2 else later:
            advance(modes_at, now)
    from_pair = lax.ppermute(strips[0], "pos", pair)
    from_next = lax.ppermute(strips[1], "pos", following)
    sums = [[keep[0], got[0]] for keep, got in blocks]

    object_out, probe_out = call(
        functools.partial(finish_kernel, [(1, 2)] * modes),
        (shape(parts, half_rows, columns), shape(parts, share, 128)),
        [],
        [probe_own, object_field, strips[2], from_pair, from_next, *sum(sums, [])],
        "finish",
    )
    probe_out = probe_out.reshape(parts, share // modes, modes, 128).transpose(0, 2, 1, 3)
    return (object_out, probe_out.reshape(parts, modes, share // modes * 128))


def solution(mesh):
    in_specs = (
        P(None, ("group", "pos"), None),
        P(None, "tile", None),
        P(("group", "pos"), None, None),
        P(("group", "pos"), None),
        P(("group", "pos")),
    )
    out_specs = (P(None, ("group", "pos", "tile"), None), P(None, ("group", "tile"), "pos"))
    return jax.shard_map(
        on_device, mesh=mesh, in_specs=in_specs, out_specs=out_specs, check_vma=False
    )
```
